32 devices in a mesh: groups: 1, tensor: 16 (over z, y, core), replica: 2 (over x).
Axes of the slice: x: 2, y: 2, z: 4, core: 2. Of those that a mesh axis runs over, the one named last changes fastest.
Arguments:
- q_latent: bfloat16 [256, 1536], P(('groups', 'tensor', 'replica')), may hold values from -6 to 6
- q_gain: float32 [1536], replicated, may hold values from 0.25 to 1.75
- q_up: bfloat16 [1536, 12288], P(None, 'tensor'), may hold values from -0.15625 to 0.15625
- w_uk: bfloat16 [64, 128, 512], P('tensor'), may hold values from -0.5 to 0.5
- w_uv: bfloat16 [64, 512, 128], P('tensor'), may hold values from -1 to 1
- w_o: bfloat16 [8192, 7168], P('tensor', 'replica'), may hold values from -0.0625 to 0.0625
- new_kv: bfloat16 [256, 576], P(('groups', 'tensor', 'replica')), may hold values from -6 to 6
- latent_cache: bfloat16 [64, 1024, 576], P(('groups', 'tensor', 'replica')), may hold values from -64 to 64
- cache_len: int32 [64], P(('groups', 'tensor', 'replica')), may hold values from 128 to 1024, as said below
- draft_count: int32 [64], P(('groups', 'tensor', 'replica')), may hold values from 1 to 4, as said below
Outputs:
- attn_out: bfloat16 [256, 7168], P(('groups', 'tensor', 'replica'))
The draws below stay inside these ranges and needn't reach their ends.
Inputs may be any that keep to these rules, and one draw needn't show every extreme that they name: `cache_len`: some request of every draw uses all 1024 slots. The first draft_count rows of a request are in use; some request of every draw uses all 4.
All inputs are finite; a program needn't handle non-finite values.
Results may differ from the reference program's by a relative error of at most 0.024.
The reference program's roundings to bfloat16 on the way count: a program that leaves them out, or rounds other values in their place, can miss the bound.
Values may be sent and summed in bfloat16 or wider, within the bound.
A program may use at most 64 MiB of HBM per device.

```python
import jax
import jax.numpy as jnp
from jax import lax

D = 7168
HEADS = 64
QLAT = 1536
LATENT = 512
ROPE = 64
NOPE = 128
VDIM = 128
CACHE = 1024
DRAFT = 4
KVW = 576
QKD = 192
REQS = 64
TOKENS = 256
N_TENSOR = 16


def draw_latent_cache(key, part):
    base_key = jax.random.fold_in(jax.random.fold_in(key, 11), 0)
    stored = jax.random.normal(base_key, (REQS, CACHE, KVW), jnp.float32)
    return jnp.clip(stored, -64.0, 64.0).astype(jnp.bfloat16)


def draw_cache_len(key, part):
    length_key, offset_key = jax.random.split(jax.random.fold_in(key, 23))
    lengths = jax.random.randint(length_key, (REQS,), CACHE // 8, CACHE + 1)
    offset = jax.random.randint(offset_key, (), 0, 7)
    filled = jnp.arange(REQS) % 7 == offset
    return jnp.where(filled, CACHE, lengths).astype(jnp.int32)


def draw_draft_count(key, part):
    count_key, offset_key = jax.random.split(jax.random.fold_in(key, 37))
    counts = jax.random.randint(count_key, (REQS,), 1, DRAFT + 1)
    offset = jax.random.randint(offset_key, (), 0, 5)
    filled = jnp.arange(REQS) % 5 == offset
    return jnp.where(filled, DRAFT, counts).astype(jnp.int32)


def shard_levels(rng, extent, shards, least, largest):
    def one(position, parts):
        draws = jax.random.uniform(jax.random.fold_in(jax.random.fold_in(rng, 6), position), (parts,), jnp.float32, least / len(shards), largest / len(shards))
        return jnp.repeat(jnp.exp(draws), extent[position] // parts).reshape((-1,) + (1,) * (len(extent) - position - 1))

    factor_of = one(*shards[0])
    for cut in shards[1:]:
        factor_of = factor_of * one(*cut)
    return factor_of


def bell_draw(rng, shape, width, bound, cuts=(), dtype=jnp.bfloat16):
    values = width * jax.random.normal(rng, shape, jnp.float32)
    if cuts:
        values = values * shard_levels(rng, shape, cuts, -0.22, 0.18)
    return jnp.clip(values, -bound, bound).astype(dtype)


def setup_inputs(seed: int = 0, part: int = 0) -> dict:
    streams_of = jax.random.split(jax.random.key(seed), 11)
    part_keys = jax.random.split(jax.random.fold_in(streams_of[10], part), 11)
    return {
        "q_latent": bell_draw(part_keys[0], (TOKENS, QLAT), 1.0, 6.0, ((0, 32),)),
        "q_gain": jnp.clip(1.0 + 0.15 * jax.random.normal(streams_of[1], (QLAT,), jnp.float32), 0.25, 1.75),
        "q_up": bell_draw(streams_of[2], (QLAT, HEADS * QKD), QLAT ** -0.5, 0.15625, ((1, 16),)),
        "w_uk": bell_draw(streams_of[3], (HEADS, NOPE, LATENT), NOPE ** -0.5, 0.5, ((0, 16),)),
        "w_uv": bell_draw(streams_of[4], (HEADS, LATENT, VDIM), (LATENT // 16) ** -0.5, 1.0, ((0, 16),)),
        "w_o": bell_draw(streams_of[5], (HEADS * VDIM, D), (HEADS * VDIM) ** -0.5, 0.0625, ((0, 16), (1, 2))),
        "new_kv": bell_draw(part_keys[6], (TOKENS, KVW), 1.0, 6.0, ((0, 32),)),
        "latent_cache": draw_latent_cache(jax.random.fold_in(jax.random.fold_in(streams_of[10], part), 71), part),
        "cache_len": draw_cache_len(jax.random.fold_in(jax.random.fold_in(streams_of[10], part), 71), part),
        "draft_count": draw_draft_count(jax.random.fold_in(jax.random.fold_in(streams_of[10], part), 71), part),
    }


rms_eps = 1e-06
rope_base = 50000.0

def normalize(rows_in, gain_row):
    values_f = rows_in.astype(jnp.float32)
    scaled = values_f * lax.rsqrt(lax.optimization_barrier(jnp.mean(values_f * values_f, axis=-1, keepdims=True)) + rms_eps)
    return (scaled * gain_row).astype(jnp.bfloat16)

def rotate(rope_part, positions):
    half_width = rope_part.shape[-1] // 2
    frequency = rope_base ** (-(jnp.arange(half_width).astype(jnp.float32) * 2.0 / rope_part.shape[-1]))
    angles = positions[:, None, None] * frequency
    cosine = jnp.cos(angles)
    sine = jnp.sin(angles)
    widened = rope_part.astype(jnp.float32)
    first_half = widened[..., :half_width]
    second_half = widened[..., half_width:]
    turned = jnp.concatenate([first_half * cosine - second_half * sine, second_half * cosine + first_half * sine], axis=-1)
    return turned.astype(jnp.bfloat16)

def attend(query_rows, new_rows, cache_rows, length, draft_total):
    queries = query_rows.reshape(-1, query_rows.shape[-1])
    contract = (((1,), (1,)), ((), ()))
    score_scale = (NOPE + ROPE) ** (-0.5)
    cache_scores = lax.dot_general(queries, cache_rows, contract, preferred_element_type=jnp.float32) * score_scale
    new_scores = lax.dot_general(queries, new_rows, contract, preferred_element_type=jnp.float32) * score_scale
    row_draft = jnp.arange(queries.shape[0]) // query_rows.shape[1]
    cache_seen = jnp.arange(cache_rows.shape[0]) < length
    new_seen = jnp.arange(new_rows.shape[0])[None, :] <= row_draft[:, None]
    cache_scores = jnp.where(cache_seen[None, :], cache_scores, -jnp.inf)
    new_scores = jnp.where(new_seen, new_scores, -jnp.inf)
    row_peak = jnp.maximum(lax.optimization_barrier(jnp.max(cache_scores, axis=1)), lax.optimization_barrier(jnp.max(new_scores, axis=1)))[:, None]
    cache_exp = jnp.exp(cache_scores - row_peak)
    new_exp = jnp.exp(new_scores - row_peak)
    denominator = lax.optimization_barrier(jnp.sum(cache_exp, axis=1, keepdims=True)) + lax.optimization_barrier(jnp.sum(new_exp, axis=1, keepdims=True))
    cache_weights = (cache_exp / denominator).astype(jnp.bfloat16)
    new_weights = (new_exp / denominator).astype(jnp.bfloat16)
    latent_mix = jnp.dot(cache_weights, cache_rows[:, :LATENT], preferred_element_type=jnp.float32)
    latent_mix = latent_mix + jnp.dot(new_weights, new_rows[:, :LATENT], preferred_element_type=jnp.float32)
    latent_mix = jnp.where((row_draft < draft_total)[:, None], latent_mix, 0.0).astype(jnp.bfloat16)
    return latent_mix.reshape(query_rows.shape[0], query_rows.shape[1], LATENT)

def reference(q_latent, q_gain, q_up, w_uk, w_uv, w_o, new_kv, latent_cache, cache_len, draft_count):
    normed = normalize(q_latent, q_gain)
    query_full = jnp.dot(normed, q_up, preferred_element_type=jnp.float32).astype(jnp.bfloat16)
    query_full = query_full.reshape(TOKENS, HEADS, QKD)
    absorbed = jnp.einsum('thn,hnl->thl', query_full[..., :NOPE].astype(jnp.float32), w_uk.astype(jnp.float32)).astype(jnp.bfloat16)
    row_length = jnp.broadcast_to(cache_len[:, None], (REQS, DRAFT)).reshape(-1)
    positions = (row_length + jnp.arange(TOKENS) % DRAFT).astype(jnp.float32)
    rotated = rotate(query_full[..., NOPE:], positions)
    query = jnp.concatenate([absorbed, rotated], axis=-1)

    def one_request(packed):
        return attend(packed[0], packed[1], packed[2], packed[3], packed[4])
    latent_out = lax.map(one_request, (query.reshape(REQS, DRAFT, HEADS, KVW), new_kv.reshape(REQS, DRAFT, KVW), latent_cache, cache_len, draft_count))
    latent_out = latent_out.reshape(TOKENS, HEADS, LATENT)
    head_values = jnp.einsum('thl,hlv->thv', latent_out.astype(jnp.float32), w_uv.astype(jnp.float32)).astype(jnp.bfloat16)
    group_width = HEADS // N_TENSOR * VDIM
    grouped_values = jnp.swapaxes(head_values.reshape(TOKENS, N_TENSOR, group_width), 0, 1)
    grouped_weights = w_o.reshape(N_TENSOR, group_width, D)

    def add_group(running, pair):
        contribution = jnp.dot(pair[0], pair[1], preferred_element_type=jnp.float32).astype(jnp.bfloat16)
        contribution = lax.optimization_barrier(contribution)
        return (running + contribution.astype(jnp.float32), None)
    running, unused = lax.scan(add_group, jnp.zeros((TOKENS, D), jnp.float32), (grouped_values, grouped_weights))
    return running.astype(jnp.bfloat16)
```

```python
import functools

import jax
import jax.numpy as jnp
from jax import lax
from jax.experimental import pallas as pl
from jax.experimental.pallas import tpu as pltpu
from jax.sharding import PartitionSpec as P

LATENT = 512
ROPE = 64
NOPE = 128
VDIM = 128
DRAFT = 4
REQ_DEV = 2
MESH = pl.DeviceIdType.MESH


rms_eps = 1e-06
rope_base = 50000.0


def normalize(rows_in, gain_row):
    values_f = rows_in.astype(jnp.float32)
    scaled = values_f * lax.rsqrt(jnp.mean(values_f * values_f, axis=-1, keepdims=True) + rms_eps)
    return (scaled * gain_row).astype(jnp.bfloat16)


def rotate(rope_part, positions):
    half_width = rope_part.shape[-1] // 2
    frequency = rope_base ** (
        -(jnp.arange(half_width).astype(jnp.float32) * 2.0 / rope_part.shape[-1])
    )
    angles = positions[:, None, None] * frequency
    cosine = jnp.cos(angles)
    sine = jnp.sin(angles)
    widened = rope_part.astype(jnp.float32)
    first_half = widened[..., :half_width]
    second_half = widened[..., half_width:]
    turned = jnp.concatenate(
        [first_half * cosine - second_half * sine, second_half * cosine + first_half * sine],
        axis=-1,
    )
    return turned.astype(jnp.bfloat16)


def attend(query_rows, new_rows, cache_rows, length, draft_total):
    queries = query_rows.reshape(-1, query_rows.shape[-1])
    contract = (((1,), (1,)), ((), ()))
    score_scale = (NOPE + ROPE) ** (-0.5)
    cache_scores = (
        lax.dot_general(queries, cache_rows, contract, preferred_element_type=jnp.float32)
        * score_scale
    )
    new_scores = (
        lax.dot_general(queries, new_rows, contract, preferred_element_type=jnp.float32)
        * score_scale
    )
    row_draft = jnp.arange(queries.shape[0]) // query_rows.shape[1]
    cache_seen = jnp.arange(cache_rows.shape[0]) < length
    new_seen = jnp.arange(new_rows.shape[0])[None, :] <= row_draft[:, None]
    cache_scores = jnp.where(cache_seen[None, :], cache_scores, -jnp.inf)
    new_scores = jnp.where(new_seen, new_scores, -jnp.inf)
    row_peak = jnp.maximum(jnp.max(cache_scores, axis=1), jnp.max(new_scores, axis=1))[:, None]
    cache_exp = jnp.exp(cache_scores - row_peak)
    new_exp = jnp.exp(new_scores - row_peak)
    denominator = jnp.sum(cache_exp, axis=1, keepdims=True) + jnp.sum(
        new_exp, axis=1, keepdims=True
    )
    cache_weights = (cache_exp / denominator).astype(jnp.bfloat16)
    new_weights = (new_exp / denominator).astype(jnp.bfloat16)
    latent_mix = jnp.dot(cache_weights, cache_rows[:, :LATENT], preferred_element_type=jnp.float32)
    latent_mix = latent_mix + jnp.dot(
        new_weights, new_rows[:, :LATENT], preferred_element_type=jnp.float32
    )
    latent_mix = jnp.where((row_draft < draft_total)[:, None], latent_mix, 0.0).astype(jnp.bfloat16)
    return latent_mix.reshape(query_rows.shape[0], query_rows.shape[1], LATENT)


def split_axis(count):
    near = 2 if count % 2 == 0 else 1
    side = 2 if (count // near) % 2 == 0 else 1
    return near, side, count // near // side


def column_chunks(width):
    for parts in (4, 3, 2):
        if width % (parts * 128) == 0:
            return parts
    return 1


def meet(partners):
    barrier = pltpu.get_barrier_semaphore()
    for partner in partners:
        pl.semaphore_signal(barrier, inc=1, device_id=partner, device_id_type=MESH)
    pl.semaphore_wait(barrier, len(partners))


def place():
    group = lax.axis_index("groups")
    me = lax.axis_index("tensor")
    copy = lax.axis_index("replica")
    return group, me, copy


def project(sizes, hv_ref, wo_ref, out_ref, spread, wo, sent1, got1, sent2, got2, kept2, sent3,
            got3, kept3, sentx, gotx, wo_sem, hs, hr, s1, r1, s2, r2, s3, r3, sx, rx):
    tensors, copies, rows_dev = sizes
    near, side, far = split_axis(tensors)
    parts = column_chunks(wo_ref.shape[1])
    width = wo_ref.shape[1] // parts
    group, me, copy = place()
    c = lax.rem(me, near)
    y = lax.rem(me // near, side)
    z = me // (near * side)

    def at(z_to, y_to, c_to):
        return (group, (z_to * side + y_to) * near + c_to, copy)

    def twin(step):
        return lax.rem(copy + step, copies)

    loads = [
        pltpu.make_async_copy(
            wo_ref.at[:, pl.ds(k * width, width)], wo.at[k], wo_sem.at[k]
        )
        for k in range(parts)
    ]
    for load in loads:
        load.start()
    near_peers = [at(z, y, lax.rem(c + d, near)) for d in range(1, near)]
    side_peers = [at(z, lax.rem(y + d, side), c) for d in range(1, side)]
    far_peers = [at(lax.rem(z + d, far), y, c) for d in range(1, far)]
    twin_peers = [(group, me, twin(d)) for d in range(1, copies)]
    meet(near_peers + side_peers + far_peers + twin_peers)

    def send(src, dst, send_sem, recv_sem, peer):
        push = pltpu.make_async_remote_copy(
            src_ref=src, dst_ref=dst, send_sem=send_sem, recv_sem=recv_sem,
            device_id=peer, device_id_type=MESH,
        )
        push.start()
        return push

    spread_out = [
        send(hv_ref, spread.at[d - 1], hs.at[d - 1], hr.at[d - 1], twin_peers[d - 1])
        for d in range(1, copies)
    ]

    pushes1, pushes2, pushes3, pushesx = {}, {}, {}, {}

    def multiply(k):
        loads[k].wait()
        weights = wo[k]
        own = jnp.dot(hv_ref[...], weights, preferred_element_type=jnp.float32)
        if k == 0:
            for push in spread_out:
                push.wait_recv()
        others = [
            jnp.dot(spread[d], weights, preferred_element_type=jnp.float32)
            for d in range(copies - 1)
        ]
        by_step = [own] + others
        if copies == 2:
            swap = copy == 1
            ordered = [jnp.where(swap, by_step[1], by_step[0]), jnp.where(swap, by_step[0], by_step[1])]
        else:
            ordered = []
            for slot in range(copies):
                chosen = by_step[0]
                for d in range(1, copies):
                    chosen = jnp.where(lax.rem(copy - d + copies, copies) == slot, by_step[d], chosen)
                ordered.append(chosen)
        for t in range(tensors):
            block = jnp.concatenate([o[t * rows_dev : (t + 1) * rows_dev] for o in ordered], axis=0)
            ct, yt, zt = t % near, (t // near) % side, t // (near * side)
            sent1[k, ct, yt, zt] = block.astype(jnp.bfloat16)
        pushes1[k] = [
            send(sent1.at[k, lax.rem(c + d, near)], got1.at[k, d - 1],
                 s1.at[k, d - 1], r1.at[k, d - 1], near_peers[d - 1])
            for d in range(1, near)
        ]

    def sum_near(k):
        for push in pushes1[k]:
            push.wait_recv()
        for d in range(side):
            to = lax.rem(y + d, side)
            total = sent1[k, c, to].astype(jnp.float32)
            for e in range(near - 1):
                total = total + got1[k, e, to].astype(jnp.float32)
            if d == 0:
                kept2[k] = total
            else:
                sent2[k, d - 1] = total.astype(jnp.bfloat16)
        pushes2[k] = [
            send(sent2.at[k, d - 1], got2.at[k, d - 1], s2.at[k, d - 1], r2.at[k, d - 1],
                 side_peers[d - 1])
            for d in range(1, side)
        ]

    def sum_side(k):
        for push in pushes2[k]:
            push.wait_recv()
        pushes3[k] = []
        for d in list(range(1, far)) + [0]:
            to = lax.rem(z + d, far)
            total = kept2[k, to]
            for e in range(side - 1):
                total = total + got2[k, e, to].astype(jnp.float32)
            if d == 0:
                kept3[k] = total
            else:
                sent3[k, d - 1] = total.astype(jnp.bfloat16)
                pushes3[k].append(
                    send(sent3.at[k, d - 1], got3.at[k, d - 1], s3.at[k, d - 1],
                         r3.at[k, d - 1], far_peers[d - 1])
                )

    def sum_far(k):
        for push in pushes3[k]:
            push.wait_recv()
        total = kept3[k]
        for e in range(far - 1):
            total = total + got3[k, e].astype(jnp.float32)
        for r in range(copies):
            sentx[k, r] = total[r * rows_dev : (r + 1) * rows_dev]
        pushesx[k] = [
            send(sentx.at[k, twin(d)], gotx.at[k, d - 1], sx.at[k, d - 1], rx.at[k, d - 1],
                 twin_peers[d - 1])
            for d in range(1, copies)
        ]
        out_ref[copy, :, k * width : (k + 1) * width] = sentx[k, copy]

    def finish(k):
        for d in range(1, copies):
            pushesx[k][d - 1].wait_recv()
            origin = lax.rem(copy - d + copies, copies)
            out_ref[origin, :, k * width : (k + 1) * width] = gotx[k, d - 1]

    stages = (multiply, sum_near, sum_side, sum_far, finish)
    for step in range(parts + len(stages) - 1):
        for depth, stage in enumerate(stages):
            if 0 <= step - depth < parts:
                stage(step - depth)
    for push in spread_out:
        push.wait_send()
    for table in (pushes1, pushes2, pushes3, pushesx):
        for k in range(parts):
            for push in table[k]:
                push.wait_send()


def project_call(head_values, w_o, tensors, copies, rows_dev):
    near, side, far = split_axis(tensors)
    parts = column_chunks(w_o.shape[1])
    width = w_o.shape[1] // parts
    block = copies * rows_dev
    bf16, f32 = jnp.bfloat16, jnp.float32
    dma = pltpu.SemaphoreType.DMA
    n1, n2, n3, nx = (max(v - 1, 1) for v in (near, side, far, copies))
    return pl.pallas_call(
        functools.partial(project, (tensors, copies, rows_dev)),
        out_shape=jax.ShapeDtypeStruct((copies, rows_dev, w_o.shape[1]), f32),
        in_specs=[pl.BlockSpec(memory_space=pltpu.VMEM), pl.BlockSpec(memory_space=pl.ANY)],
        out_specs=pl.BlockSpec(memory_space=pltpu.VMEM),
        scratch_shapes=[
            pltpu.VMEM((nx,) + head_values.shape, bf16),
            pltpu.VMEM((parts, w_o.shape[0], width), bf16),
            pltpu.VMEM((parts, near, side, far, block, width), bf16),
            pltpu.VMEM((parts, n1, side, far, block, width), bf16),
            pltpu.VMEM((parts, n2, far, block, width), bf16),
            pltpu.VMEM((parts, n2, far, block, width), bf16),
            pltpu.VMEM((parts, far, block, width), f32),
            pltpu.VMEM((parts, n3, block, width), bf16),
            pltpu.VMEM((parts, n3, block, width), bf16),
            pltpu.VMEM((parts, block, width), f32),
            pltpu.VMEM((parts, copies, rows_dev, width), f32),
            pltpu.VMEM((parts, nx, rows_dev, width), f32),
            dma((parts,)),
            dma((nx,)), dma((nx,)),
            dma((parts, n1)), dma((parts, n1)),
            dma((parts, n2)), dma((parts, n2)),
            dma((parts, n3)), dma((parts, n3)),
            dma((parts, nx)), dma((parts, nx)),
        ],
        compiler_params=pltpu.CompilerParams(
            collective_id=3, has_side_effects=True, vmem_limit_bytes=48 * 1024 * 1024
        ),
    )(head_values, w_o)


def shards(q_latent, q_gain, q_up, w_uk, w_uv, w_o, new_kv, latent_cache, cache_len, draft_count):
    rows_dev = q_latent.shape[0]
    owners = lax.axis_size("tensor")
    heads_dev = w_uk.shape[0]
    head_count = heads_dev * owners
    normed = normalize(q_latent, q_gain)
    query_full = jnp.dot(
        lax.all_gather(normed, "tensor", axis=0, tiled=True),
        q_up,
        preferred_element_type=jnp.float32,
    ).astype(jnp.bfloat16)
    query_full = query_full.reshape(owners, rows_dev, heads_dev, NOPE + ROPE)
    absorbed = jnp.einsum(
        "pihn,hnl->iphl", query_full[..., :NOPE], w_uk, preferred_element_type=jnp.float32
    ).astype(jnp.bfloat16)
    rope_part = jnp.swapaxes(query_full[..., NOPE:], 0, 1)
    packed_queries = jnp.concatenate([absorbed, rope_part], axis=-1).reshape(
        rows_dev, owners, heads_dev * (LATENT + ROPE)
    )
    arrived = lax.all_to_all(packed_queries, "tensor", split_axis=1, concat_axis=1, tiled=True)
    arrived = arrived.reshape(rows_dev, head_count, LATENT + ROPE)
    row_length = jnp.broadcast_to(cache_len[:, None], (REQ_DEV, DRAFT)).reshape(-1)
    positions = (row_length + jnp.arange(rows_dev) % DRAFT).astype(jnp.float32)
    rotated = rotate(arrived[..., LATENT:], positions)
    query = jnp.concatenate([arrived[..., :LATENT], rotated], axis=-1)
    latent_out = jax.vmap(attend)(
        query.reshape(REQ_DEV, DRAFT, head_count, LATENT + ROPE),
        new_kv.reshape(REQ_DEV, DRAFT, LATENT + ROPE),
        latent_cache,
        cache_len,
        draft_count,
    )
    latent_out = latent_out.reshape(rows_dev, owners, heads_dev * LATENT)
    returned = lax.all_to_all(latent_out, "tensor", split_axis=1, concat_axis=1, tiled=True)
    returned = returned.reshape(rows_dev, owners, heads_dev, LATENT)
    head_values = jnp.einsum(
        "ithl,hlv->tihv", returned, w_uv, preferred_element_type=jnp.float32
    ).astype(jnp.bfloat16)
    head_values = head_values.reshape(owners * rows_dev, heads_dev * VDIM)
    replicas = lax.axis_size("replica")
    placed = project_call(head_values, w_o, owners, replicas, rows_dev)
    placed = jnp.swapaxes(placed, 0, 1).reshape(rows_dev, replicas * w_o.shape[1])
    return placed.astype(jnp.bfloat16)


def solution(mesh):
    return jax.shard_map(
        shards,
        mesh=mesh,
        in_specs=(
            P(("groups", "tensor", "replica"), None),
            P(),
            P(None, "tensor"),
            P("tensor", None, None),
            P("tensor", None, None),
            P("tensor", "replica"),
            P(("groups", "tensor", "replica"), None),
            P(("groups", "tensor", "replica"), None, None),
            P(("groups", "tensor", "replica")),
            P(("groups", "tensor", "replica")),
        ),
        out_specs=P(("groups", "tensor", "replica"), None),
        check_vma=False,
    )
```

```python
import functools

import jax
import jax.numpy as jnp
from jax import lax
from jax.experimental import pallas as pl
from jax.experimental.pallas import tpu as pltpu
from jax.sharding import PartitionSpec as P

LATENT = 512
ROPE = 64
NOPE = 128
VDIM = 128
DRAFT = 4
REQ_DEV = 2
MESH = pl.DeviceIdType.MESH


rms_eps = 1e-06
rope_base = 50000.0


def split_axis(count):
    near = 2 if count % 2 == 0 else 1
    side = 2 if (count // near) % 2 == 0 else 1
    return near, side, count // near // side


def column_chunks(width):
    for parts in (4, 3, 2):
        if width % (parts * 128) == 0:
            return parts
    return 1


def meet(partners):
    barrier = pltpu.get_barrier_semaphore()
    for partner in partners:
        pl.semaphore_signal(barrier, inc=1, device_id=partner, device_id_type=MESH)
    pl.semaphore_wait(barrier, len(partners))


def place():
    group = lax.axis_index("groups")
    me = lax.axis_index("tensor")
    copy = lax.axis_index("replica")
    return group, me, copy


def project(sizes, hv_ref, wo_ref, out_ref, spread, wo, sent1, got1, sent2, got2, kept2, sent3,
            got3, kept3, sentx, gotx, wo_sem, hs, hr, s1, r1, s2, r2, s3, r3, sx, rx):
    tensors, copies, rows_dev = sizes
    near, side, far = split_axis(tensors)
    parts = column_chunks(wo_ref.shape[1])
    width = wo_ref.shape[1] // parts
    group, me, copy = place()
    c = lax.rem(me, near)
    y = lax.rem(me // near, side)
    z = me // (near * side)

    def at(z_to, y_to, c_to):
        return (group, (z_to * side + y_to) * near + c_to, copy)

    def twin(step):
        return lax.rem(copy + step, copies)

    loads = [
        pltpu.make_async_copy(
            wo_ref.at[:, pl.ds(k * width, width)], wo.at[k], wo_sem.at[k]
        )
        for k in range(parts)
    ]
    for load in loads:
        load.start()
    near_peers = [at(z, y, lax.rem(c + d, near)) for d in range(1, near)]
    side_peers = [at(z, lax.rem(y + d, side), c) for d in range(1, side)]
    far_peers = [at(lax.rem(z + d, far), y, c) for d in range(1, far)]
    twin_peers = [(group, me, twin(d)) for d in range(1, copies)]
    meet(near_peers + side_peers + far_peers + twin_peers)

    def send(src, dst, send_sem, recv_sem, peer):
        push = pltpu.make_async_remote_copy(
            src_ref=src, dst_ref=dst, send_sem=send_sem, recv_sem=recv_sem,
            device_id=peer, device_id_type=MESH,
        )
        push.start()
        return push

    spread_out = [
        send(hv_ref, spread.at[d - 1], hs.at[d - 1], hr.at[d - 1], twin_peers[d - 1])
        for d in range(1, copies)
    ]

    pushes1, pushes2, pushes3, pushesx = {}, {}, {}, {}

    def multiply(k):
        loads[k].wait()
        weights = wo[k]
        own = jnp.dot(hv_ref[...], weights, preferred_element_type=jnp.float32)
        if k == 0:
            for push in spread_out:
                push.wait_recv()
        others = [
            jnp.dot(spread[d], weights, preferred_element_type=jnp.float32)
            for d in range(copies - 1)
        ]
        by_step = [own] + others
        if copies == 2:
            swap = copy == 1
            ordered = [jnp.where(swap, by_step[1], by_step[0]), jnp.where(swap, by_step[0], by_step[1])]
        else:
            ordered = []
            for slot in range(copies):
                chosen = by_step[0]
                for d in range(1, copies):
                    chosen = jnp.where(lax.rem(copy - d + copies, copies) == slot, by_step[d], chosen)
                ordered.append(chosen)
        for t in range(tensors):
            block = jnp.concatenate([o[t * rows_dev : (t + 1) * rows_dev] for o in ordered], axis=0)
            ct, yt, zt = t % near, (t // near) % side, t // (near * side)
            sent1[k, ct, yt, zt] = block.astype(jnp.bfloat16)
        pushes1[k] = [
            send(sent1.at[k, lax.rem(c + d, near)], got1.at[k, d - 1],
                 s1.at[k, d - 1], r1.at[k, d - 1], near_peers[d - 1])
            for d in range(1, near)
        ]

    def sum_near(k):
        for push in pushes1[k]:
            push.wait_recv()
        for d in range(side):
            to = lax.rem(y + d, side)
            total = sent1[k, c, to].astype(jnp.float32)
            for e in range(near - 1):
                total = total + got1[k, e, to].astype(jnp.float32)
            if d == 0:
                kept2[k] = total
            else:
                sent2[k, d - 1] = total.astype(jnp.bfloat16)
        pushes2[k] = [
            send(sent2.at[k, d - 1], got2.at[k, d - 1], s2.at[k, d - 1], r2.at[k, d - 1],
                 side_peers[d - 1])
            for d in range(1, side)
        ]

    def sum_side(k):
        for push in pushes2[k]:
            push.wait_recv()
        pushes3[k] = []
        for d in list(range(1, far)) + [0]:
            to = lax.rem(z + d, far)
            total = kept2[k, to]
            for e in range(side - 1):
                total = total + got2[k, e, to].astype(jnp.float32)
            if d == 0:
                kept3[k] = total
            else:
                sent3[k, d - 1] = total.astype(jnp.bfloat16)
                pushes3[k].append(
                    send(sent3.at[k, d - 1], got3.at[k, d - 1], s3.at[k, d - 1],
                         r3.at[k, d - 1], far_peers[d - 1])
                )

    def sum_far(k):
        for push in pushes3[k]:
            push.wait_recv()
        total = kept3[k]
        for e in range(far - 1):
            total = total + got3[k, e].astype(jnp.float32)
        for r in range(copies):
            sentx[k, r] = total[r * rows_dev : (r + 1) * rows_dev]
        pushesx[k] = [
            send(sentx.at[k, twin(d)], gotx.at[k, d - 1], sx.at[k, d - 1], rx.at[k, d - 1],
                 twin_peers[d - 1])
            for d in range(1, copies)
        ]
        out_ref[copy, :, k * width : (k + 1) * width] = sentx[k, copy]

    def finish(k):
        for d in range(1, copies):
            pushesx[k][d - 1].wait_recv()
            origin = lax.rem(copy - d + copies, copies)
            out_ref[origin, :, k * width : (k + 1) * width] = gotx[k, d - 1]

    stages = (multiply, sum_near, sum_side, sum_far, finish)
    for step in range(parts + len(stages) - 1):
        for depth, stage in enumerate(stages):
            if 0 <= step - depth < parts:
                stage(step - depth)
    for push in spread_out:
        push.wait_send()
    for table in (pushes1, pushes2, pushes3, pushesx):
        for k in range(parts):
            for push in table[k]:
                push.wait_send()


def project_call(head_values, w_o, tensors, copies, rows_dev):
    near, side, far = split_axis(tensors)
    parts = column_chunks(w_o.shape[1])
    width = w_o.shape[1] // parts
    block = copies * rows_dev
    bf16, f32 = jnp.bfloat16, jnp.float32
    dma = pltpu.SemaphoreType.DMA
    n1, n2, n3, nx = (max(v - 1, 1) for v in (near, side, far, copies))
    return pl.pallas_call(
        functools.partial(project, (tensors, copies, rows_dev)),
        out_shape=jax.ShapeDtypeStruct((copies, rows_dev, w_o.shape[1]), f32),
        in_specs=[pl.BlockSpec(memory_space=pltpu.VMEM), pl.BlockSpec(memory_space=pl.ANY)],
        out_specs=pl.BlockSpec(memory_space=pltpu.VMEM),
        scratch_shapes=[
            pltpu.VMEM((nx,) + head_values.shape, bf16),
            pltpu.VMEM((parts, w_o.shape[0], width), bf16),
            pltpu.VMEM((parts, near, side, far, block, width), bf16),
            pltpu.VMEM((parts, n1, side, far, block, width), bf16),
            pltpu.VMEM((parts, n2, far, block, width), bf16),
            pltpu.VMEM((parts, n2, far, block, width), bf16),
            pltpu.VMEM((parts, far, block, width), f32),
            pltpu.VMEM((parts, n3, block, width), bf16),
            pltpu.VMEM((parts, n3, block, width), bf16),
            pltpu.VMEM((parts, block, width), f32),
            pltpu.VMEM((parts, copies, rows_dev, width), f32),
            pltpu.VMEM((parts, nx, rows_dev, width), f32),
            dma((parts,)),
            dma((nx,)), dma((nx,)),
            dma((parts, n1)), dma((parts, n1)),
            dma((parts, n2)), dma((parts, n2)),
            dma((parts, n3)), dma((parts, n3)),
            dma((parts, nx)), dma((parts, nx)),
        ],
        compiler_params=pltpu.CompilerParams(
            collective_id=3, has_side_effects=True, vmem_limit_bytes=48 * 1024 * 1024
        ),
    )(head_values, w_o)


def paired(first, second, low):
    rows = first.shape[0]
    zero = jnp.where(low, first, pltpu.roll(second, DRAFT, 0))
    one = jnp.where(low, pltpu.roll(first, rows - DRAFT, 0), second)
    return zero, one


def mix(sizes, ql_ref, gain_ref, nk_ref, cos_ref, sin_ref, len_ref, count_ref, qup_hbm, wuk_hbm,
        wuv_hbm, cache_hbm, hv_ref, qup, wuk, wuv, cache, gathered, qsend, rsend, qgot, rgot, lsend,
        lgot, load_sem, fs, fr, ys, yr, ns, nr, qs, qr, rs, rr, ls, lr):
    tensors = sizes
    near, side, far = split_axis(tensors)
    heads_dev = wuk.shape[0]
    rows_dev = ql_ref.shape[0]
    rows = tensors * rows_dev
    half = ql_ref.shape[1] // 2
    group, me, copy = place()
    c = lax.rem(me, near)
    y = lax.rem(me // near, side)
    z = me // (near * side)
    f32, bf16 = jnp.float32, jnp.bfloat16

    loads = [
        pltpu.make_async_copy(src, dst, load_sem.at[n])
        for n, (src, dst) in enumerate(
            ((qup_hbm, qup), (wuk_hbm, wuk), (cache_hbm, cache), (wuv_hbm, wuv))
        )
    ]
    for load in loads:
        load.start()

    def peer(step):
        return lax.rem(me + step, tensors)

    def at(z_to, y_to, c_to):
        return (group, (z_to * side + y_to) * near + c_to, copy)

    def send(src, dst, send_sem, recv_sem, to):
        push = pltpu.make_async_remote_copy(
            src_ref=src, dst_ref=dst, send_sem=send_sem, recv_sem=recv_sem,
            device_id=to, device_id_type=MESH,
        )
        push.start()
        return push

    values = ql_ref[...].astype(f32)
    scaled = values * lax.rsqrt(jnp.mean(values * values, axis=-1, keepdims=True) + rms_eps)
    normed = scaled * gain_ref[...]
    gathered[c, y, z] = jnp.concatenate([normed[:, :half], normed[:, half:]], axis=0).astype(bf16)
    meet([(group, peer(d), copy) for d in range(1, tensors)])

    far_out = [
        send(gathered.at[c, y, z], gathered.at[c, y, z], fs.at[d - 1], fr.at[d - 1],
             at(lax.rem(z + d, far), y, c))
        for d in range(1, far)
    ]
    for push in far_out:
        push.wait_recv()
    side_out = [
        send(gathered.at[c, y], gathered.at[c, y], ys.at[d - 1], yr.at[d - 1],
             at(z, lax.rem(y + d, side), c))
        for d in range(1, side)
    ]
    for push in side_out:
        push.wait_recv()
    near_out = [
        send(gathered.at[c], gathered.at[c], ns.at[d - 1], nr.at[d - 1],
             at(z, y, lax.rem(c + d, near)))
        for d in range(1, near)
    ]
    loads[0].wait()
    loads[1].wait()
    for push in near_out:
        push.wait_recv()

    everyone = gathered[...].astype(f32).reshape(tensors, 2 * rows_dev, half)
    left = everyone[:, :rows_dev].reshape(rows, half).astype(bf16)
    right = everyone[:, rows_dev:].reshape(rows, half).astype(bf16)
    query = jnp.dot(left, qup[:half], preferred_element_type=f32)
    query = query + jnp.dot(right, qup[half:], preferred_element_type=f32)
    query = query.astype(bf16).astype(f32)
    low = lax.broadcasted_iota(jnp.int32, (rows, 1), 0) % rows_dev < DRAFT
    qkd = NOPE + ROPE
    nope_pairs, rope_pairs = [], []
    for h in range(0, heads_dev, 2):
        here, there = h * qkd, (h + 1) * qkd
        nope_pairs.append(
            paired(query[:, here : here + NOPE], query[:, there : there + NOPE], low)
        )
        zero, one = paired(
            query[:, here + NOPE : here + qkd], query[:, there + NOPE : there + qkd], low
        )
        rope_pairs.append(jnp.concatenate([zero, one], axis=1).reshape(tensors, rows_dev, 2 * ROPE))
    rsend[...] = jnp.concatenate(rope_pairs, axis=1).astype(bf16)

    def slot(to):
        return (lax.rem(to, near) * side + lax.rem(to // near, side)) * far + to // (near * side)

    mine = slot(me)
    rope_out, query_out, latent_out = [], [], []
    for r in range(REQ_DEV):
        tiles = []
        for n, pair in enumerate(nope_pairs):
            tile = pair[r].astype(bf16)
            first = jnp.dot(tile, wuk[2 * n], preferred_element_type=f32)
            second = jnp.dot(tile, wuk[2 * n + 1], preferred_element_type=f32)
            tiles.append(jnp.where(low, first, second).reshape(tensors, rows_dev, LATENT))
        qsend[:, r] = jnp.concatenate(tiles, axis=1).astype(bf16)
        for d in range(1, tensors):
            to = peer(d)
            if r == 0:
                rope_out.append(
                    send(rsend.at[slot(to)], rgot.at[me], rs.at[d - 1], rr.at[d - 1],
                         (group, to, copy))
                )
            query_out.append(
                send(qsend.at[slot(to), r], qgot.at[me, r], qs.at[r, d - 1], qr.at[r, d - 1],
                     (group, to, copy))
            )
        qgot[me, r] = qsend[mine, r]
    rgot[me] = rsend[mine]

    pad = 128 - nk_ref.shape[0]
    fresh = jnp.concatenate(
        [nk_ref[...].astype(f32), jnp.zeros((pad, nk_ref.shape[1]), f32)], axis=0
    ).astype(bf16)
    fresh_latent, fresh_rope = fresh[:, :LATENT], fresh[:, LATENT:]
    scale = qkd ** (-0.5)
    total = tensors * heads_dev * DRAFT
    slots = cache.shape[2]
    row_draft = lax.broadcasted_iota(jnp.int32, (total, 1), 0) % DRAFT
    fresh_column = lax.broadcasted_iota(jnp.int32, (1, 128), 1)
    cache_column = lax.broadcasted_iota(jnp.int32, (1, slots), 1)
    for push in rope_out:
        push.wait_recv()
    rope = rgot[...].astype(f32).reshape(total // rows_dev, rows_dev, 2 * ROPE)
    rope2 = rope.reshape(total, 2 * ROPE)
    lane = lax.broadcasted_iota(jnp.int32, (1, 2 * ROPE), 1) % ROPE
    swapped = jnp.where(
        lane < ROPE // 2,
        pltpu.roll(rope2, 2 * ROPE - ROPE // 2, 1),
        pltpu.roll(rope2, ROPE // 2, 1),
    ).reshape(rope.shape)
    turned = (rope * cos_ref[...][None] + swapped * sin_ref[...][None]).astype(bf16)
    turned = turned.reshape(total, 2 * ROPE)
    loads[2].wait()
    transposed = (((1,), (1,)), ((), ()))
    for r in range(REQ_DEV):
        for push in query_out[r * (tensors - 1) : (r + 1) * (tensors - 1)]:
            push.wait_recv()
        absorbed = qgot[:, r].reshape(total, LATENT)
        rotated = turned[:, r * ROPE : (r + 1) * ROPE]
        scores = jnp.dot(absorbed, cache[r, :LATENT], preferred_element_type=f32)
        scores = (scores + jnp.dot(rotated, cache[r, LATENT:], preferred_element_type=f32)) * scale
        fresh_scores = lax.dot_general(
            absorbed, fresh_latent, transposed, preferred_element_type=f32
        )
        fresh_scores = (
            fresh_scores
            + lax.dot_general(rotated, fresh_rope, transposed, preferred_element_type=f32)
        ) * scale
        scores = jnp.where(cache_column < len_ref[r], scores, -jnp.inf)
        begin = r * DRAFT
        seen = (fresh_column >= begin) & (fresh_column - begin <= row_draft)
        fresh_scores = jnp.where(seen, fresh_scores, -jnp.inf)
        peak = jnp.maximum(
            jnp.max(scores, axis=1, keepdims=True), jnp.max(fresh_scores, axis=1, keepdims=True)
        )
        powers = jnp.exp(scores - peak)
        fresh_powers = jnp.exp(fresh_scores - peak)
        denominator = jnp.sum(powers, axis=1, keepdims=True) + jnp.sum(
            fresh_powers, axis=1, keepdims=True
        )
        weights = (powers / denominator).astype(bf16)
        fresh_weights = (fresh_powers / denominator).astype(bf16)
        latents = lax.dot_general(
            weights, cache[r, :LATENT], transposed, preferred_element_type=f32
        )
        latents = latents + jnp.dot(fresh_weights, fresh_latent, preferred_element_type=f32)
        latents = jnp.where(row_draft < count_ref[r], latents, 0.0)
        lsend[:, r] = latents.astype(bf16).reshape(tensors, heads_dev * DRAFT, LATENT)
        for d in range(1, tensors):
            to = peer(d)
            latent_out.append(
                send(lsend.at[to, r], lgot.at[me, r], ls.at[r, d - 1], lr.at[r, d - 1],
                     (group, to, copy))
            )
        lgot[me, r] = lsend[me, r]
    loads[3].wait()
    halves = []
    for r in range(REQ_DEV):
        for push in latent_out[r * (tensors - 1) : (r + 1) * (tensors - 1)]:
            push.wait_recv()
        back = lgot[:, r].astype(f32)
        parts = []
        for n in range(heads_dev // 2):
            tile = back[:, n * rows_dev : (n + 1) * rows_dev].reshape(rows, LATENT).astype(bf16)
            first = jnp.dot(tile, wuv[2 * n], preferred_element_type=f32)
            second = jnp.dot(tile, wuv[2 * n + 1], preferred_element_type=f32)
            parts.append(jnp.where(low, first, second))
        halves.append(parts)
    for n in range(heads_dev // 2):
        for h, block in enumerate(paired(halves[0][n], halves[1][n], low)):
            start = (2 * n + h) * VDIM
            hv_ref[:, start : start + VDIM] = block.astype(bf16)
    for push in far_out + side_out + near_out + rope_out + query_out + latent_out:
        push.wait_send()


def mix_call(q_latent, q_gain, q_up, w_uk, w_uv, new_kv, latent_cache, cache_len, draft_count, tensors):
    near, side, far = split_axis(tensors)
    rows_dev, width = q_latent.shape
    heads_dev = w_uk.shape[0]
    bf16, f32 = jnp.bfloat16, jnp.float32
    dma = pltpu.SemaphoreType.DMA
    n1, n2, n3 = (max(v - 1, 1) for v in (near, side, far))
    tall = heads_dev * DRAFT
    cache = jnp.swapaxes(latent_cache, 1, 2)
    frequency = rope_base ** (-(jnp.arange(ROPE // 2).astype(f32) * 2.0 / ROPE))
    positions = (cache_len[:, None] + jnp.arange(DRAFT)).astype(f32)
    angles = positions[:, :, None] * frequency
    cosine, sine = jnp.cos(angles), jnp.sin(angles)
    cosine = jnp.concatenate([cosine, cosine], axis=-1)
    sine = jnp.concatenate([-sine, sine], axis=-1)
    lay = lambda a: jnp.tile(jnp.swapaxes(a, 0, 1).reshape(DRAFT, REQ_DEV * ROPE), (2, 1))
    vmem = pl.BlockSpec(memory_space=pltpu.VMEM)
    smem = pl.BlockSpec(memory_space=pltpu.SMEM)
    hbm = pl.BlockSpec(memory_space=pl.ANY)
    exchange = (REQ_DEV, tensors - 1)
    return pl.pallas_call(
        functools.partial(mix, tensors),
        out_shape=jax.ShapeDtypeStruct((tensors * rows_dev, heads_dev * VDIM), bf16),
        in_specs=[vmem] * 5 + [smem] * 2 + [hbm] * 4,
        out_specs=vmem,
        scratch_shapes=[
            pltpu.VMEM(q_up.shape, bf16),
            pltpu.VMEM(w_uk.shape, bf16),
            pltpu.VMEM(w_uv.shape, bf16),
            pltpu.VMEM(cache.shape, bf16),
            pltpu.VMEM((near, side, far, 2 * rows_dev, width // 2), bf16),
            pltpu.VMEM((tensors, REQ_DEV, tall, LATENT), bf16),
            pltpu.VMEM((tensors, tall, 2 * ROPE), bf16),
            pltpu.VMEM((tensors, REQ_DEV, tall, LATENT), bf16),
            pltpu.VMEM((tensors, tall, 2 * ROPE), bf16),
            pltpu.VMEM((tensors, REQ_DEV, tall, LATENT), bf16),
            pltpu.VMEM((tensors, REQ_DEV, tall, LATENT), bf16),
            dma((4,)),
            dma((n3,)), dma((n3,)),
            dma((n2,)), dma((n2,)),
            dma((n1,)), dma((n1,)),
            dma(exchange), dma(exchange),
            dma((tensors - 1,)), dma((tensors - 1,)),
            dma(exchange), dma(exchange),
        ],
        compiler_params=pltpu.CompilerParams(
            collective_id=1, has_side_effects=True, vmem_limit_bytes=48 * 1024 * 1024
        ),
    )(q_latent, q_gain[None], new_kv, lay(cosine), lay(sine), cache_len, draft_count,
      q_up, w_uk, w_uv, cache)


def shards(q_latent, q_gain, q_up, w_uk, w_uv, w_o, new_kv, latent_cache, cache_len, draft_count):
    rows_dev = q_latent.shape[0]
    owners = lax.axis_size("tensor")
    head_values = mix_call(
        q_latent, q_gain, q_up, w_uk, w_uv, new_kv, latent_cache, cache_len, draft_count, owners
    )
    replicas = lax.axis_size("replica")
    placed = project_call(head_values, w_o, owners, replicas, rows_dev)
    placed = jnp.swapaxes(placed, 0, 1).reshape(rows_dev, replicas * w_o.shape[1])
    return placed.astype(jnp.bfloat16)


def solution(mesh):
    return jax.shard_map(
        shards,
        mesh=mesh,
        in_specs=(
            P(("groups", "tensor", "replica"), None),
            P(),
            P(None, "tensor"),
            P("tensor", None, None),
            P("tensor", None, None),
            P("tensor", "replica"),
            P(("groups", "tensor", "replica"), None),
            P(("groups", "tensor", "replica"), None, None),
            P(("groups", "tensor", "replica")),
            P(("groups", "tensor", "replica")),
        ),
        out_specs=P(("groups", "tensor", "replica"), None),
        check_vma=False,
    )
```

```python
import functools
import math

import jax
import jax.numpy as jnp
from jax import lax
from jax.experimental import pallas as pl
from jax.experimental.pallas import tpu as pltpu
from jax.sharding import PartitionSpec as P

LATENT = 512
ROPE = 64
NOPE = 128
VDIM = 128
DRAFT = 4
REQ_DEV = 2
MESH = pl.DeviceIdType.MESH


rms_eps = 1e-06
rope_base = 50000.0


def split_axis(count):
    near = 2 if count % 2 == 0 else 1
    side = 2 if (count // near) % 2 == 0 else 1
    return near, side, count // near // side


def column_chunks(width):
    for parts in (7, 4, 3, 2):
        if width % (parts * 128) == 0:
            return parts
    return 1


def meet(partners):
    barrier = pltpu.get_barrier_semaphore()
    for partner in partners:
        pl.semaphore_signal(barrier, inc=1, device_id=partner, device_id_type=MESH)
    pl.semaphore_wait(barrier, len(partners))


def place():
    group = lax.axis_index("groups")
    me = lax.axis_index("tensor")
    copy = lax.axis_index("replica")
    return group, me, copy


def project(sizes, loads, hv_ref, wo_ref, out_ref, spread, wo, sent1, got1, sent2, got2, kept2, sent3,
            got3, kept3, sentx, gotx, hs, hr, s1, r1, s2, r2, s3, r3, sx, rx):
    tensors, copies, rows_dev = sizes
    near, side, far = split_axis(tensors)
    parts = column_chunks(wo_ref.shape[1])
    width = wo_ref.shape[1] // parts
    group, me, copy = place()
    c = lax.rem(me, near)
    y = lax.rem(me // near, side)
    z = me // (near * side)

    def at(z_to, y_to, c_to):
        return (group, (z_to * side + y_to) * near + c_to, copy)

    def twin(step):
        return lax.rem(copy + step, copies)

    near_peers = [at(z, y, lax.rem(c + d, near)) for d in range(1, near)]
    side_peers = [at(z, lax.rem(y + d, side), c) for d in range(1, side)]
    far_peers = [at(lax.rem(z + d, far), y, c) for d in range(1, far)]
    twin_peers = [(group, me, twin(d)) for d in range(1, copies)]
    def send(src, dst, send_sem, recv_sem, peer):
        push = pltpu.make_async_remote_copy(
            src_ref=src, dst_ref=dst, send_sem=send_sem, recv_sem=recv_sem,
            device_id=peer, device_id_type=MESH,
        )
        push.start()
        return push

    spread_out = [
        send(hv_ref, spread.at[d - 1], hs.at[d - 1], hr.at[d - 1], twin_peers[d - 1])
        for d in range(1, copies)
    ]

    pushes1, pushes2, pushes3, pushesx = {}, {}, {}, {}

    def multiply(k):
        loads[k].wait()
        weights = wo[k]
        own = jnp.dot(hv_ref[...], weights, preferred_element_type=jnp.float32)
        if k == 0:
            for push in spread_out:
                push.wait_recv()
        others = [
            jnp.dot(spread[d], weights, preferred_element_type=jnp.float32)
            for d in range(copies - 1)
        ]
        by_step = [own] + others
        if copies == 2:
            swap = copy == 1
            ordered = [jnp.where(swap, by_step[1], by_step[0]), jnp.where(swap, by_step[0], by_step[1])]
        else:
            ordered = []
            for slot in range(copies):
                chosen = by_step[0]
                for d in range(1, copies):
                    chosen = jnp.where(lax.rem(copy - d + copies, copies) == slot, by_step[d], chosen)
                ordered.append(chosen)
        for t in range(tensors):
            block = jnp.concatenate([o[t * rows_dev : (t + 1) * rows_dev] for o in ordered], axis=0)
            ct, yt, zt = t % near, (t // near) % side, t // (near * side)
            sent1[k, ct, yt, zt] = block.astype(jnp.bfloat16)
        pushes1[k] = [
            send(sent1.at[k, lax.rem(c + d, near)], got1.at[k, d - 1],
                 s1.at[k, d - 1], r1.at[k, d - 1], near_peers[d - 1])
            for d in range(1, near)
        ]

    def sum_near(k):
        for push in pushes1[k]:
            push.wait_recv()
        for d in range(side):
            to = lax.rem(y + d, side)
            total = sent1[k, c, to].astype(jnp.float32)
            for e in range(near - 1):
                total = total + got1[k, e, to].astype(jnp.float32)
            if d == 0:
                kept2[k] = total
            else:
                sent2[k, d - 1] = total.astype(jnp.bfloat16)
        pushes2[k] = [
            send(sent2.at[k, d - 1], got2.at[k, d - 1], s2.at[k, d - 1], r2.at[k, d - 1],
                 side_peers[d - 1])
            for d in range(1, side)
        ]

    def sum_side(k):
        for push in pushes2[k]:
            push.wait_recv()
        pushes3[k] = []
        for d in list(range(1, far)) + [0]:
            to = lax.rem(z + d, far)
            total = kept2[k, to]
            for e in range(side - 1):
                total = total + got2[k, e, to].astype(jnp.float32)
            if d == 0:
                kept3[k] = total
            else:
                sent3[k, d - 1] = total.astype(jnp.bfloat16)
                pushes3[k].append(
                    send(sent3.at[k, d - 1], got3.at[k, d - 1], s3.at[k, d - 1],
                         r3.at[k, d - 1], far_peers[d - 1])
                )

    def sum_far(k):
        for push in pushes3[k]:
            push.wait_recv()
        total = kept3[k]
        for e in range(far - 1):
            total = total + got3[k, e].astype(jnp.float32)
        for r in range(copies):
            sentx[k, r] = total[r * rows_dev : (r + 1) * rows_dev]
        pushesx[k] = [
            send(sentx.at[k, twin(d)], gotx.at[k, d - 1], sx.at[k, d - 1], rx.at[k, d - 1],
                 twin_peers[d - 1])
            for d in range(1, copies)
        ]
        out_ref[copy, :, k * width : (k + 1) * width] = sentx[k, copy]

    def finish(k):
        for d in range(1, copies):
            pushesx[k][d - 1].wait_recv()
            origin = lax.rem(copy - d + copies, copies)
            out_ref[origin, :, k * width : (k + 1) * width] = gotx[k, d - 1]

    stages = (multiply, sum_near, sum_side, sum_far, finish)
    for step in range(parts + len(stages) - 1):
        for depth, stage in enumerate(stages):
            if 0 <= step - depth < parts:
                stage(step - depth)
    for push in spread_out:
        push.wait_send()
    for table in (pushes1, pushes2, pushes3, pushesx):
        for k in range(parts):
            for push in table[k]:
                push.wait_send()


def project_scratch(hv_shape, wo_shape, tensors, copies, rows_dev):
    near, side, far = split_axis(tensors)
    parts = column_chunks(wo_shape[1])
    width = wo_shape[1] // parts
    block = copies * rows_dev
    bf16, f32 = jnp.bfloat16, jnp.float32
    dma = pltpu.SemaphoreType.DMA
    n1, n2, n3, nx = (max(v - 1, 1) for v in (near, side, far, copies))
    return [
            pltpu.VMEM((nx,) + hv_shape, bf16),
            pltpu.VMEM((parts, wo_shape[0], width), bf16),
            pltpu.VMEM((parts, near, side, far, block, width), bf16),
            pltpu.VMEM((parts, n1, side, far, block, width), bf16),
            pltpu.VMEM((parts, n2, far, block, width), bf16),
            pltpu.VMEM((parts, n2, far, block, width), bf16),
            pltpu.VMEM((parts, far, block, width), f32),
            pltpu.VMEM((parts, n3, block, width), bf16),
            pltpu.VMEM((parts, n3, block, width), bf16),
            pltpu.VMEM((parts, block, width), f32),
            pltpu.VMEM((parts, copies, rows_dev, width), f32),
            pltpu.VMEM((parts, nx, rows_dev, width), f32),
            dma((nx,)), dma((nx,)),
            dma((parts, n1)), dma((parts, n1)),
            dma((parts, n2)), dma((parts, n2)),
            dma((parts, n3)), dma((parts, n3)),
            dma((parts, nx)), dma((parts, nx)),
    ]


def paired(first, second, low):
    rows = first.shape[0]
    zero = jnp.where(low, first, pltpu.roll(second, DRAFT, 0))
    one = jnp.where(low, pltpu.roll(first, rows - DRAFT, 0), second)
    return zero, one


def mix(sizes, gain_ref, ql_ref, nk_ref, len_ref, count_ref, qup_hbm, wuk_hbm, wuv_hbm, cache_hbm,
        wo_hbm, out_ref, qup, wuk, wuv, cache, hv_ref, gathered,
        qsend, rsend, qgot, rgot, lsend, lgot, load_sem, wo_sem, fs, fr, ys, yr, ns, nr, qs, qr, rs,
        rr, ls, lr, *rest):
    tensors, copies, rows_dev = sizes
    near, side, far = split_axis(tensors)
    heads_dev = wuk.shape[0]
    rows = tensors * rows_dev
    half = ql_ref.shape[1] // 2
    group, me, copy = place()
    c = lax.rem(me, near)
    y = lax.rem(me // near, side)
    z = me // (near * side)
    f32, bf16 = jnp.float32, jnp.bfloat16

    loads = [
        pltpu.make_async_copy(src, dst, load_sem.at[n])
        for n, (src, dst) in enumerate(
            ((qup_hbm, qup), (wuk_hbm, wuk), (cache_hbm, cache), (wuv_hbm, wuv))
        )
    ]
    wo = rest[1]
    width = wo.shape[2]
    wo_loads = [
        pltpu.make_async_copy(wo_hbm.at[:, pl.ds(k * width, width)], wo.at[k], wo_sem.at[k])
        for k in range(wo.shape[0])
    ]
    for load in loads + wo_loads:
        load.start()

    def peer(step):
        return lax.rem(me + step, tensors)

    def at(z_to, y_to, c_to):
        return (group, (z_to * side + y_to) * near + c_to, copy)

    def send(src, dst, send_sem, recv_sem, to):
        push = pltpu.make_async_remote_copy(
            src_ref=src, dst_ref=dst, send_sem=send_sem, recv_sem=recv_sem,
            device_id=to, device_id_type=MESH,
        )
        push.start()
        return push

    values = ql_ref[...].astype(f32)
    scaled = values * lax.rsqrt(jnp.mean(values * values, axis=-1, keepdims=True) + rms_eps)
    normed = scaled * gain_ref[...]
    gathered[c, y, z] = jnp.concatenate([normed[:, :half], normed[:, half:]], axis=0).astype(bf16)
    meet(
        [(group, peer(d), copy) for d in range(1, tensors)]
        + [(group, me, lax.rem(copy + d, copies)) for d in range(1, copies)]
    )

    far_out = [
        send(gathered.at[c, y, z], gathered.at[c, y, z], fs.at[d - 1], fr.at[d - 1],
             at(lax.rem(z + d, far), y, c))
        for d in range(1, far)
    ]
    column = lax.broadcasted_iota(jnp.int32, (rows_dev, 2 * ROPE), 1)
    table_draft = lax.broadcasted_iota(jnp.int32, (rows_dev, 2 * ROPE), 0) % DRAFT
    fraction = (column % (ROPE // 2)).astype(f32) * 2.0 / ROPE
    frequency = jnp.exp(fraction * -math.log(rope_base))
    length = jnp.where(column < ROPE, len_ref[0], len_ref[1])
    angle = (length + table_draft).astype(f32) * frequency
    cosine = jnp.cos(angle)
    sine = jnp.sin(angle)
    sine = jnp.where(column % ROPE < ROPE // 2, -sine, sine)
    for push in far_out:
        push.wait_recv()
    side_out = [
        send(gathered.at[c, y], gathered.at[c, y], ys.at[d - 1], yr.at[d - 1],
             at(z, lax.rem(y + d, side), c))
        for d in range(1, side)
    ]
    for push in side_out:
        push.wait_recv()
    near_out = [
        send(gathered.at[c], gathered.at[c], ns.at[d - 1], nr.at[d - 1],
             at(z, y, lax.rem(c + d, near)))
        for d in range(1, near)
    ]
    loads[0].wait()
    loads[1].wait()
    for push in near_out:
        push.wait_recv()

    everyone = gathered[...].astype(f32).reshape(tensors, 2 * rows_dev, half)
    left = everyone[:, :rows_dev].reshape(rows, half).astype(bf16)
    right = everyone[:, rows_dev:].reshape(rows, half).astype(bf16)
    query = jnp.dot(left, qup[:half], preferred_element_type=f32)
    query = query + jnp.dot(right, qup[half:], preferred_element_type=f32)
    query = query.astype(bf16).astype(f32)
    low = lax.broadcasted_iota(jnp.int32, (rows, 1), 0) % rows_dev < DRAFT
    qkd = NOPE + ROPE
    nope_pairs, rope_pairs = [], []
    for h in range(0, heads_dev, 2):
        here, there = h * qkd, (h + 1) * qkd
        nope_pairs.append(
            paired(query[:, here : here + NOPE], query[:, there : there + NOPE], low)
        )
        zero, one = paired(
            query[:, here + NOPE : here + qkd], query[:, there + NOPE : there + qkd], low
        )
        rope_pairs.append(jnp.concatenate([zero, one], axis=1).reshape(tensors, rows_dev, 2 * ROPE))
    rsend[...] = jnp.concatenate(rope_pairs, axis=1).astype(bf16)

    def slot(to):
        return (lax.rem(to, near) * side + lax.rem(to // near, side)) * far + to // (near * side)

    mine = slot(me)
    rope_out, query_out, latent_out = [], [], []
    for r in range(REQ_DEV):
        tiles = []
        for n, pair in enumerate(nope_pairs):
            tile = pair[r].astype(bf16)
            first = jnp.dot(tile, wuk[2 * n], preferred_element_type=f32)
            second = jnp.dot(tile, wuk[2 * n + 1], preferred_element_type=f32)
            tiles.append(jnp.where(low, first, second).reshape(tensors, rows_dev, LATENT))
        qsend[:, r] = jnp.concatenate(tiles, axis=1).astype(bf16)
        for d in range(1, tensors):
            to = peer(d)
            if r == 0:
                rope_out.append(
                    send(rsend.at[slot(to)], rgot.at[me], rs.at[d - 1], rr.at[d - 1],
                         (group, to, copy))
                )
            query_out.append(
                send(qsend.at[slot(to), r], qgot.at[me, r], qs.at[r, d - 1], qr.at[r, d - 1],
                     (group, to, copy))
            )
        qgot[me, r] = qsend[mine, r]
    rgot[me] = rsend[mine]

    pad = 128 - nk_ref.shape[0]
    fresh = jnp.concatenate(
        [nk_ref[...].astype(f32), jnp.zeros((pad, nk_ref.shape[1]), f32)], axis=0
    ).astype(bf16)
    fresh_latent, fresh_rope = fresh[:, :LATENT], fresh[:, LATENT:]
    scale = qkd ** (-0.5)
    total = tensors * heads_dev * DRAFT
    slots = cache.shape[2]
    row_draft = lax.broadcasted_iota(jnp.int32, (total, 1), 0) % DRAFT
    fresh_column = lax.broadcasted_iota(jnp.int32, (1, 128), 1)
    cache_column = lax.broadcasted_iota(jnp.int32, (1, slots), 1)
    for push in rope_out:
        push.wait_recv()
    rope = rgot[...].astype(f32).reshape(total // rows_dev, rows_dev, 2 * ROPE)
    rope2 = rope.reshape(total, 2 * ROPE)
    lane = lax.broadcasted_iota(jnp.int32, (1, 2 * ROPE), 1) % ROPE
    swapped = jnp.where(
        lane < ROPE // 2,
        pltpu.roll(rope2, 2 * ROPE - ROPE // 2, 1),
        pltpu.roll(rope2, ROPE // 2, 1),
    ).reshape(rope.shape)
    turned = (rope * cosine[None] + swapped * sine[None]).astype(bf16)
    turned = turned.reshape(total, 2 * ROPE)
    loads[2].wait()
    transposed = (((1,), (1,)), ((), ()))
    for r in range(REQ_DEV):
        for push in query_out[r * (tensors - 1) : (r + 1) * (tensors - 1)]:
            push.wait_recv()
        absorbed = qgot[:, r].reshape(total, LATENT)
        rotated = turned[:, r * ROPE : (r + 1) * ROPE]
        scores = jnp.dot(absorbed, cache[r, :LATENT], preferred_element_type=f32)
        scores = (scores + jnp.dot(rotated, cache[r, LATENT:], preferred_element_type=f32)) * scale
        fresh_scores = lax.dot_general(
            absorbed, fresh_latent, transposed, preferred_element_type=f32
        )
        fresh_scores = (
            fresh_scores
            + lax.dot_general(rotated, fresh_rope, transposed, preferred_element_type=f32)
        ) * scale
        scores = jnp.where(cache_column < len_ref[r], scores, -jnp.inf)
        begin = r * DRAFT
        seen = (fresh_column >= begin) & (fresh_column - begin <= row_draft)
        fresh_scores = jnp.where(seen, fresh_scores, -jnp.inf)
        peak = jnp.maximum(
            jnp.max(scores, axis=1, keepdims=True), jnp.max(fresh_scores, axis=1, keepdims=True)
        )
        powers = jnp.exp(scores - peak)
        fresh_powers = jnp.exp(fresh_scores - peak)
        denominator = jnp.sum(powers, axis=1, keepdims=True) + jnp.sum(
            fresh_powers, axis=1, keepdims=True
        )
        weights = (powers / denominator).astype(bf16)
        fresh_weights = (fresh_powers / denominator).astype(bf16)
        latents = lax.dot_general(
            weights, cache[r, :LATENT], transposed, preferred_element_type=f32
        )
        latents = latents + jnp.dot(fresh_weights, fresh_latent, preferred_element_type=f32)
        latents = jnp.where(row_draft < count_ref[r], latents, 0.0)
        lsend[:, r] = latents.astype(bf16).reshape(tensors, heads_dev * DRAFT, LATENT)
        for d in range(1, tensors):
            to = peer(d)
            latent_out.append(
                send(lsend.at[to, r], lgot.at[me, r], ls.at[r, d - 1], lr.at[r, d - 1],
                     (group, to, copy))
            )
        lgot[me, r] = lsend[me, r]
    loads[3].wait()
    halves = []
    for r in range(REQ_DEV):
        for push in latent_out[r * (tensors - 1) : (r + 1) * (tensors - 1)]:
            push.wait_recv()
        back = lgot[:, r].astype(f32)
        parts = []
        for n in range(heads_dev // 2):
            tile = back[:, n * rows_dev : (n + 1) * rows_dev].reshape(rows, LATENT).astype(bf16)
            first = jnp.dot(tile, wuv[2 * n], preferred_element_type=f32)
            second = jnp.dot(tile, wuv[2 * n + 1], preferred_element_type=f32)
            parts.append(jnp.where(low, first, second))
        halves.append(parts)
    for n in range(heads_dev // 2):
        for h, block in enumerate(paired(halves[0][n], halves[1][n], low)):
            start = (2 * n + h) * VDIM
            hv_ref[:, start : start + VDIM] = block.astype(bf16)
    project(sizes, wo_loads, hv_ref, wo_hbm, out_ref, *rest)
    for push in far_out + side_out + near_out + rope_out + query_out + latent_out:
        push.wait_send()


def mix_call(q_latent, q_gain, q_up, w_uk, w_uv, w_o, new_kv, latent_cache, cache_len, draft_count,
             tensors, copies):
    near, side, far = split_axis(tensors)
    rows_dev, width = q_latent.shape
    heads_dev = w_uk.shape[0]
    bf16, f32 = jnp.bfloat16, jnp.float32
    dma = pltpu.SemaphoreType.DMA
    n1, n2, n3 = (max(v - 1, 1) for v in (near, side, far))
    tall = heads_dev * DRAFT
    cache = jnp.swapaxes(latent_cache, 1, 2)
    vmem = pl.BlockSpec(memory_space=pltpu.VMEM)
    hbm = pl.BlockSpec(memory_space=pltpu.HBM)
    hv_shape = (tensors * rows_dev, heads_dev * VDIM)
    exchange = (REQ_DEV, tensors - 1)
    return pl.pallas_call(
        functools.partial(mix, (tensors, copies, rows_dev)),
        out_shape=jax.ShapeDtypeStruct((copies, rows_dev, w_o.shape[1]), f32),
        in_specs=[vmem] * 3 + [pl.BlockSpec(memory_space=pltpu.SMEM)] * 2 + [hbm] * 5,
        out_specs=vmem,
        scratch_shapes=[
            pltpu.VMEM(q_up.shape, bf16),
            pltpu.VMEM(w_uk.shape, bf16),
            pltpu.VMEM(w_uv.shape, bf16),
            pltpu.VMEM(cache.shape, bf16),
            pltpu.VMEM(hv_shape, bf16),
            pltpu.VMEM((near, side, far, 2 * rows_dev, width // 2), bf16),
            pltpu.VMEM((tensors, REQ_DEV, tall, LATENT), bf16),
            pltpu.VMEM((tensors, tall, 2 * ROPE), bf16),
            pltpu.VMEM((tensors, REQ_DEV, tall, LATENT), bf16),
            pltpu.VMEM((tensors, tall, 2 * ROPE), bf16),
            pltpu.VMEM((tensors, REQ_DEV, tall, LATENT), bf16),
            pltpu.VMEM((tensors, REQ_DEV, tall, LATENT), bf16),
            dma((4,)),
            dma((column_chunks(w_o.shape[1]),)),
            dma((n3,)), dma((n3,)),
            dma((n2,)), dma((n2,)),
            dma((n1,)), dma((n1,)),
            dma(exchange), dma(exchange),
            dma((tensors - 1,)), dma((tensors - 1,)),
            dma(exchange), dma(exchange),
        ]
        + project_scratch(hv_shape, w_o.shape, tensors, copies, rows_dev),
        compiler_params=pltpu.CompilerParams(
            collective_id=1, has_side_effects=True, vmem_limit_bytes=56 * 1024 * 1024
        ),
    )(q_gain[None], q_latent, new_kv, cache_len, draft_count, q_up, w_uk, w_uv, cache, w_o)


def shards(q_latent, q_gain, q_up, w_uk, w_uv, w_o, new_kv, latent_cache, cache_len, draft_count):
    rows_dev = q_latent.shape[0]
    owners = lax.axis_size("tensor")
    replicas = lax.axis_size("replica")
    placed = mix_call(
        q_latent, q_gain, q_up, w_uk, w_uv, w_o, new_kv, latent_cache, cache_len, draft_count,
        owners, replicas
    )
    placed = jnp.swapaxes(placed, 0, 1).reshape(rows_dev, replicas * w_o.shape[1])
    return placed.astype(jnp.bfloat16)


def solution(mesh):
    return jax.shard_map(
        shards,
        mesh=mesh,
        in_specs=(
            P(("groups", "tensor", "replica"), None),
            P(),
            P(None, "tensor"),
            P("tensor", None, None),
            P("tensor", None, None),
            P("tensor", "replica"),
            P(("groups", "tensor", "replica"), None),
            P(("groups", "tensor", "replica"), None, None),
            P(("groups", "tensor", "replica")),
            P(("groups", "tensor", "replica")),
        ),
        out_specs=P(("groups", "tensor", "replica"), None),
        check_vma=False,
    )
```

```python
import functools
import math

import jax
import jax.numpy as jnp
from jax import lax
from jax.experimental import pallas as pl
from jax.experimental.pallas import tpu as pltpu
from jax.sharding import PartitionSpec as P

LATENT = 512
ROPE = 64
NOPE = 128
VDIM = 128
DRAFT = 4
REQ_DEV = 2
MESH = pl.DeviceIdType.MESH


rms_eps = 1e-06
rope_base = 50000.0


def split_axis(count):
    near = 2 if count % 2 == 0 else 1
    side = 2 if (count // near) % 2 == 0 else 1
    return near, side, count // near // side


def column_chunks(width):
    for parts in (4, 3, 2):
        if width % (parts * 128) == 0:
            return parts
    return 1


def meet(partners):
    barrier = pltpu.get_barrier_semaphore()
    for partner in partners:
        pl.semaphore_signal(barrier, inc=1, device_id=partner, device_id_type=MESH)
    pl.semaphore_wait(barrier, len(partners))


def place():
    group = lax.axis_index("groups")
    me = lax.axis_index("tensor")
    copy = lax.axis_index("replica")
    return group, me, copy


def project(sizes, loads, hv_ref, wo_ref, out_ref, spread, wo, sent1, got1, sent2, got2, kept2, sent3,
            got3, kept3, sentx, gotx, hs, hr, s1, r1, s2, r2, s3, r3, sx, rx):
    tensors, copies, rows_dev = sizes
    near, side, far = split_axis(tensors)
    parts = column_chunks(wo_ref.shape[1])
    width = wo_ref.shape[1] // parts
    group, me, copy = place()
    c = lax.rem(me, near)
    y = lax.rem(me // near, side)
    z = me // (near * side)

    def at(z_to, y_to, c_to):
        return (group, (z_to * side + y_to) * near + c_to, copy)

    def twin(step):
        return lax.rem(copy + step, copies)

    near_peers = [at(z, y, lax.rem(c + d, near)) for d in range(1, near)]
    side_peers = [at(z, lax.rem(y + d, side), c) for d in range(1, side)]
    far_peers = [at(lax.rem(z + d, far), y, c) for d in range(1, far)]
    twin_peers = [(group, me, twin(d)) for d in range(1, copies)]
    def send(src, dst, send_sem, recv_sem, peer):
        push = pltpu.make_async_remote_copy(
            src_ref=src, dst_ref=dst, send_sem=send_sem, recv_sem=recv_sem,
            device_id=peer, device_id_type=MESH,
        )
        push.start()
        return push

    spread_out = [
        send(hv_ref, spread.at[d - 1], hs.at[d - 1], hr.at[d - 1], twin_peers[d - 1])
        for d in range(1, copies)
    ]

    pushes1, pushes2, pushes3, pushesx = {}, {}, {}, {}

    def multiply(k):
        loads[k].wait()
        weights = wo[k]
        own = jnp.dot(hv_ref[...], weights, preferred_element_type=jnp.float32)
        if k == 0:
            for push in spread_out:
                push.wait_recv()
        others = [
            jnp.dot(spread[d], weights, preferred_element_type=jnp.float32)
            for d in range(copies - 1)
        ]
        by_step = [own] + others
        if copies == 2:
            swap = copy == 1
            ordered = [jnp.where(swap, by_step[1], by_step[0]), jnp.where(swap, by_step[0], by_step[1])]
        else:
            ordered = []
            for slot in range(copies):
                chosen = by_step[0]
                for d in range(1, copies):
                    chosen = jnp.where(lax.rem(copy - d + copies, copies) == slot, by_step[d], chosen)
                ordered.append(chosen)
        for t in range(tensors):
            block = jnp.concatenate([o[t * rows_dev : (t + 1) * rows_dev] for o in ordered], axis=0)
            ct, yt, zt = t % near, (t // near) % side, t // (near * side)
            sent1[k, ct, yt, zt] = block.astype(jnp.bfloat16)
        pushes1[k] = [
            send(sent1.at[k, lax.rem(c + d, near)], got1.at[k, d - 1],
                 s1.at[k, d - 1], r1.at[k, d - 1], near_peers[d - 1])
            for d in range(1, near)
        ]

    def sum_near(k):
        for push in pushes1[k]:
            push.wait_recv()
        for d in range(side):
            to = lax.rem(y + d, side)
            total = sent1[k, c, to].astype(jnp.float32)
            for e in range(near - 1):
                total = total + got1[k, e, to].astype(jnp.float32)
            if d == 0:
                kept2[k] = total
            else:
                sent2[k, d - 1] = total.astype(jnp.bfloat16)
        pushes2[k] = [
            send(sent2.at[k, d - 1], got2.at[k, d - 1], s2.at[k, d - 1], r2.at[k, d - 1],
                 side_peers[d - 1])
            for d in range(1, side)
        ]

    def sum_side(k):
        for push in pushes2[k]:
            push.wait_recv()
        pushes3[k] = []
        for d in list(range(1, far)) + [0]:
            to = lax.rem(z + d, far)
            total = kept2[k, to]
            for e in range(side - 1):
                total = total + got2[k, e, to].astype(jnp.float32)
            if d == 0:
                kept3[k] = total
            else:
                sent3[k, d - 1] = total.astype(jnp.bfloat16)
                pushes3[k].append(
                    send(sent3.at[k, d - 1], got3.at[k, d - 1], s3.at[k, d - 1],
                         r3.at[k, d - 1], far_peers[d - 1])
                )

    def sum_far(k):
        for push in pushes3[k]:
            push.wait_recv()
        total = kept3[k]
        for e in range(far - 1):
            total = total + got3[k, e].astype(jnp.float32)
        for r in range(copies):
            sentx[k, r] = total[r * rows_dev : (r + 1) * rows_dev]
        pushesx[k] = [
            send(sentx.at[k, twin(d)], gotx.at[k, d - 1], sx.at[k, d - 1], rx.at[k, d - 1],
                 twin_peers[d - 1])
            for d in range(1, copies)
        ]
        out_ref[copy, :, k * width : (k + 1) * width] = sentx[k, copy]

    def finish(k):
        for d in range(1, copies):
            pushesx[k][d - 1].wait_recv()
            origin = lax.rem(copy - d + copies, copies)
            out_ref[origin, :, k * width : (k + 1) * width] = gotx[k, d - 1]

    stages = (multiply, sum_near, sum_side, sum_far, finish)
    for step in range(parts + len(stages) - 1):
        for depth, stage in enumerate(stages):
            if 0 <= step - depth < parts:
                stage(step - depth)
    for push in spread_out:
        push.wait_send()
    for table in (pushes1, pushes2, pushes3, pushesx):
        for k in range(parts):
            for push in table[k]:
                push.wait_send()


def project_scratch(hv_shape, wo_shape, tensors, copies, rows_dev):
    near, side, far = split_axis(tensors)
    parts = column_chunks(wo_shape[1])
    width = wo_shape[1] // parts
    block = copies * rows_dev
    bf16, f32 = jnp.bfloat16, jnp.float32
    dma = pltpu.SemaphoreType.DMA
    n1, n2, n3, nx = (max(v - 1, 1) for v in (near, side, far, copies))
    return [
            pltpu.VMEM((nx,) + hv_shape, bf16),
            pltpu.VMEM((parts, wo_shape[0], width), bf16),
            pltpu.VMEM((parts, near, side, far, block, width), bf16),
            pltpu.VMEM((parts, n1, side, far, block, width), bf16),
            pltpu.VMEM((parts, n2, far, block, width), bf16),
            pltpu.VMEM((parts, n2, far, block, width), bf16),
            pltpu.VMEM((parts, far, block, width), f32),
            pltpu.VMEM((parts, n3, block, width), bf16),
            pltpu.VMEM((parts, n3, block, width), bf16),
            pltpu.VMEM((parts, block, width), f32),
            pltpu.VMEM((parts, copies, rows_dev, width), f32),
            pltpu.VMEM((parts, nx, rows_dev, width), f32),
            dma((nx,)), dma((nx,)),
            dma((parts, n1)), dma((parts, n1)),
            dma((parts, n2)), dma((parts, n2)),
            dma((parts, n3)), dma((parts, n3)),
            dma((parts, nx)), dma((parts, nx)),
    ]


def paired(first, second, low):
    rows = first.shape[0]
    zero = jnp.where(low, first, pltpu.roll(second, DRAFT, 0))
    one = jnp.where(low, pltpu.roll(first, rows - DRAFT, 0), second)
    return zero, one


def mix(sizes, gain_ref, ql_ref, nk_ref, len_ref, count_ref, qup_hbm, wuk_hbm, wuv_hbm, cache_hbm,
        wo_hbm, out_ref, qup, wuk, wuv, cache, hv_ref, gathered,
        qsend, rsend, qgot, rgot, lsend, lgot, load_sem, wo_sem, fs, fr, ys, yr, ns, nr, qs, qr, rs,
        rr, ls, lr, *rest):
    tensors, copies, rows_dev = sizes
    near, side, far = split_axis(tensors)
    heads_dev = wuk.shape[0]
    rows = tensors * rows_dev
    half = ql_ref.shape[1] // 2
    group, me, copy = place()
    c = lax.rem(me, near)
    y = lax.rem(me // near, side)
    z = me // (near * side)
    f32, bf16 = jnp.float32, jnp.bfloat16

    loads = [
        pltpu.make_async_copy(src, dst, load_sem.at[n])
        for n, (src, dst) in enumerate(
            ((qup_hbm, qup), (wuk_hbm, wuk), (cache_hbm, cache), (wuv_hbm, wuv))
        )
    ]
    wo = rest[1]
    width = wo.shape[2]
    wo_loads = [
        pltpu.make_async_copy(wo_hbm.at[:, pl.ds(k * width, width)], wo.at[k], wo_sem.at[k])
        for k in range(wo.shape[0])
    ]
    for load in loads + wo_loads:
        load.start()

    def peer(step):
        return lax.rem(me + step, tensors)

    def at(z_to, y_to, c_to):
        return (group, (z_to * side + y_to) * near + c_to, copy)

    def send(src, dst, send_sem, recv_sem, to):
        push = pltpu.make_async_remote_copy(
            src_ref=src, dst_ref=dst, send_sem=send_sem, recv_sem=recv_sem,
            device_id=to, device_id_type=MESH,
        )
        push.start()
        return push

    values = ql_ref[...].astype(f32)
    scaled = values * lax.rsqrt(jnp.mean(values * values, axis=-1, keepdims=True) + rms_eps)
    normed = scaled * gain_ref[...].reshape(1, 2 * half)
    gathered[c, y, z] = jnp.concatenate([normed[:, :half], normed[:, half:]], axis=0).astype(bf16)
    meet(
        [(group, peer(d), copy) for d in range(1, tensors)]
        + [(group, me, lax.rem(copy + d, copies)) for d in range(1, copies)]
    )

    far_out = [
        send(gathered.at[c, y, z], gathered.at[c, y, z], fs.at[d - 1], fr.at[d - 1],
             at(lax.rem(z + d, far), y, c))
        for d in range(1, far)
    ]
    column = lax.broadcasted_iota(jnp.int32, (rows_dev, 2 * ROPE), 1)
    table_draft = lax.broadcasted_iota(jnp.int32, (rows_dev, 2 * ROPE), 0) % DRAFT
    fraction = (column % (ROPE // 2)).astype(f32) * 2.0 / ROPE
    frequency = jnp.exp(fraction * -math.log(rope_base))
    length = jnp.where(column < ROPE, len_ref[0], len_ref[1])
    angle = (length + table_draft).astype(f32) * frequency
    cosine = jnp.cos(angle)
    sine = jnp.sin(angle)
    sine = jnp.where(column % ROPE < ROPE // 2, -sine, sine)
    for push in far_out:
        push.wait_recv()
    side_out = [
        send(gathered.at[c, y], gathered.at[c, y], ys.at[d - 1], yr.at[d - 1],
             at(z, lax.rem(y + d, side), c))
        for d in range(1, side)
    ]
    for push in side_out:
        push.wait_recv()
    near_out = [
        send(gathered.at[c], gathered.at[c], ns.at[d - 1], nr.at[d - 1],
             at(z, y, lax.rem(c + d, near)))
        for d in range(1, near)
    ]
    loads[0].wait()
    loads[1].wait()
    for push in near_out:
        push.wait_recv()

    everyone = gathered[...].astype(f32).reshape(tensors, 2 * rows_dev, half)
    left = everyone[:, :rows_dev].reshape(rows, half).astype(bf16)
    right = everyone[:, rows_dev:].reshape(rows, half).astype(bf16)
    query = jnp.dot(left, qup[:half], preferred_element_type=f32)
    query = query + jnp.dot(right, qup[half:], preferred_element_type=f32)
    query = query.astype(bf16).astype(f32)
    low = lax.broadcasted_iota(jnp.int32, (rows, 1), 0) % rows_dev < DRAFT
    qkd = NOPE + ROPE
    nope_pairs, rope_pairs = [], []
    for h in range(0, heads_dev, 2):
        here, there = h * qkd, (h + 1) * qkd
        nope_pairs.append(
            paired(query[:, here : here + NOPE], query[:, there : there + NOPE], low)
        )
        zero, one = paired(
            query[:, here + NOPE : here + qkd], query[:, there + NOPE : there + qkd], low
        )
        rope_pairs.append(jnp.concatenate([zero, one], axis=1).reshape(tensors, rows_dev, 2 * ROPE))
    rsend[...] = jnp.concatenate(rope_pairs, axis=1).astype(bf16)

    def slot(to):
        return (lax.rem(to, near) * side + lax.rem(to // near, side)) * far + to // (near * side)

    mine = slot(me)
    rope_out, query_out, latent_out = [], [], []
    for r in range(REQ_DEV):
        tiles = []
        for n, pair in enumerate(nope_pairs):
            tile = pair[r].astype(bf16)
            first = jnp.dot(tile, wuk[2 * n], preferred_element_type=f32)
            second = jnp.dot(tile, wuk[2 * n + 1], preferred_element_type=f32)
            tiles.append(jnp.where(low, first, second).reshape(tensors, rows_dev, LATENT))
        qsend[:, r] = jnp.concatenate(tiles, axis=1).astype(bf16)
        for d in range(1, tensors):
            to = peer(d)
            if r == 0:
                rope_out.append(
                    send(rsend.at[slot(to)], rgot.at[me], rs.at[d - 1], rr.at[d - 1],
                         (group, to, copy))
                )
            query_out.append(
                send(qsend.at[slot(to), r], qgot.at[me, r], qs.at[r, d - 1], qr.at[r, d - 1],
                     (group, to, copy))
            )
        qgot[me, r] = qsend[mine, r]
    rgot[me] = rsend[mine]

    pad = 128 - nk_ref.shape[0]
    fresh = jnp.concatenate(
        [nk_ref[...].astype(f32), jnp.zeros((pad, nk_ref.shape[1]), f32)], axis=0
    ).astype(bf16)
    fresh_latent, fresh_rope = fresh[:, :LATENT], fresh[:, LATENT:]
    scale = qkd ** (-0.5)
    total = tensors * heads_dev * DRAFT
    slots = cache.shape[2]
    row_draft = lax.broadcasted_iota(jnp.int32, (total, 1), 0) % DRAFT
    fresh_column = lax.broadcasted_iota(jnp.int32, (1, 128), 1)
    cache_column = lax.broadcasted_iota(jnp.int32, (1, slots), 1)
    for push in rope_out:
        push.wait_recv()
    rope = rgot[...].astype(f32).reshape(total // rows_dev, rows_dev, 2 * ROPE)
    rope2 = rope.reshape(total, 2 * ROPE)
    lane = lax.broadcasted_iota(jnp.int32, (1, 2 * ROPE), 1) % ROPE
    swapped = jnp.where(
        lane < ROPE // 2,
        pltpu.roll(rope2, 2 * ROPE - ROPE // 2, 1),
        pltpu.roll(rope2, ROPE // 2, 1),
    ).reshape(rope.shape)
    turned = (rope * cosine[None] + swapped * sine[None]).astype(bf16)
    turned = turned.reshape(total, 2 * ROPE)
    loads[2].wait()
    transposed = (((1,), (1,)), ((), ()))
    for r in range(REQ_DEV):
        for push in query_out[r * (tensors - 1) : (r + 1) * (tensors - 1)]:
            push.wait_recv()
        absorbed = qgot[:, r].reshape(total, LATENT)
        rotated = turned[:, r * ROPE : (r + 1) * ROPE]
        scores = jnp.dot(absorbed, cache[r, :LATENT], preferred_element_type=f32)
        scores = (scores + jnp.dot(rotated, cache[r, LATENT:], preferred_element_type=f32)) * scale
        fresh_scores = lax.dot_general(
            absorbed, fresh_latent, transposed, preferred_element_type=f32
        )
        fresh_scores = (
            fresh_scores
            + lax.dot_general(rotated, fresh_rope, transposed, preferred_element_type=f32)
        ) * scale
        scores = jnp.where(cache_column < len_ref[r], scores, -jnp.inf)
        begin = r * DRAFT
        seen = (fresh_column >= begin) & (fresh_column - begin <= row_draft)
        fresh_scores = jnp.where(seen, fresh_scores, -jnp.inf)
        peak = jnp.maximum(
            jnp.max(scores, axis=1, keepdims=True), jnp.max(fresh_scores, axis=1, keepdims=True)
        )
        powers = jnp.exp(scores - peak)
        fresh_powers = jnp.exp(fresh_scores - peak)
        denominator = jnp.sum(powers, axis=1, keepdims=True) + jnp.sum(
            fresh_powers, axis=1, keepdims=True
        )
        weights = (powers / denominator).astype(bf16)
        fresh_weights = (fresh_powers / denominator).astype(bf16)
        latents = lax.dot_general(
            weights, cache[r, :LATENT], transposed, preferred_element_type=f32
        )
        latents = latents + jnp.dot(fresh_weights, fresh_latent, preferred_element_type=f32)
        latents = jnp.where(row_draft < count_ref[r], latents, 0.0)
        lsend[:, r] = latents.astype(bf16).reshape(tensors, heads_dev * DRAFT, LATENT)
        for d in range(1, tensors):
            to = peer(d)
            latent_out.append(
                send(lsend.at[to, r], lgot.at[me, r], ls.at[r, d - 1], lr.at[r, d - 1],
                     (group, to, copy))
            )
        lgot[me, r] = lsend[me, r]
    loads[3].wait()
    halves = []
    for r in range(REQ_DEV):
        for push in latent_out[r * (tensors - 1) : (r + 1) * (tensors - 1)]:
            push.wait_recv()
        back = lgot[:, r].astype(f32)
        parts = []
        for n in range(heads_dev // 2):
            tile = back[:, n * rows_dev : (n + 1) * rows_dev].reshape(rows, LATENT).astype(bf16)
            first = jnp.dot(tile, wuv[2 * n], preferred_element_type=f32)
            second = jnp.dot(tile, wuv[2 * n + 1], preferred_element_type=f32)
            parts.append(jnp.where(low, first, second))
        halves.append(parts)
    for n in range(heads_dev // 2):
        for h, block in enumerate(paired(halves[0][n], halves[1][n], low)):
            start = (2 * n + h) * VDIM
            hv_ref[:, start : start + VDIM] = block.astype(bf16)
    project(sizes, wo_loads, hv_ref, wo_hbm, out_ref, *rest)
    for push in far_out + side_out + near_out + rope_out + query_out + latent_out:
        push.wait_send()


def mix_call(q_latent, q_gain, q_up, w_uk, w_uv, w_o, new_kv, latent_cache, cache_len, draft_count,
             tensors, copies):
    near, side, far = split_axis(tensors)
    rows_dev, width = q_latent.shape
    heads_dev = w_uk.shape[0]
    bf16, f32 = jnp.bfloat16, jnp.float32
    dma = pltpu.SemaphoreType.DMA
    n1, n2, n3 = (max(v - 1, 1) for v in (near, side, far))
    tall = heads_dev * DRAFT
    cache = jnp.swapaxes(latent_cache, 1, 2)
    vmem = pl.BlockSpec(memory_space=pltpu.VMEM)
    hbm = pl.BlockSpec(memory_space=pltpu.HBM)
    hv_shape = (tensors * rows_dev, heads_dev * VDIM)
    exchange = (REQ_DEV, tensors - 1)
    return pl.pallas_call(
        functools.partial(mix, (tensors, copies, rows_dev)),
        out_shape=jax.ShapeDtypeStruct((copies, rows_dev, w_o.shape[1]), f32),
        in_specs=[vmem] * 3 + [pl.BlockSpec(memory_space=pltpu.SMEM)] * 2 + [hbm] * 5,
        out_specs=vmem,
        scratch_shapes=[
            pltpu.VMEM(q_up.shape, bf16),
            pltpu.VMEM(w_uk.shape, bf16),
            pltpu.VMEM(w_uv.shape, bf16),
            pltpu.VMEM(cache.shape, bf16),
            pltpu.VMEM(hv_shape, bf16),
            pltpu.VMEM((near, side, far, 2 * rows_dev, width // 2), bf16),
            pltpu.VMEM((tensors, REQ_DEV, tall, LATENT), bf16),
            pltpu.VMEM((tensors, tall, 2 * ROPE), bf16),
            pltpu.VMEM((tensors, REQ_DEV, tall, LATENT), bf16),
            pltpu.VMEM((tensors, tall, 2 * ROPE), bf16),
            pltpu.VMEM((tensors, REQ_DEV, tall, LATENT), bf16),
            pltpu.VMEM((tensors, REQ_DEV, tall, LATENT), bf16),
            dma((4,)),
            dma((column_chunks(w_o.shape[1]),)),
            dma((n3,)), dma((n3,)),
            dma((n2,)), dma((n2,)),
            dma((n1,)), dma((n1,)),
            dma(exchange), dma(exchange),
            dma((tensors - 1,)), dma((tensors - 1,)),
            dma(exchange), dma(exchange),
        ]
        + project_scratch(hv_shape, w_o.shape, tensors, copies, rows_dev),
        compiler_params=pltpu.CompilerParams(
            collective_id=1, has_side_effects=True, vmem_limit_bytes=56 * 1024 * 1024
        ),
    )(q_gain, q_latent, new_kv, cache_len, draft_count, q_up, w_uk, w_uv, cache, w_o)


def shards(q_latent, q_gain, q_up, w_uk, w_uv, w_o, new_kv, latent_cache, cache_len, draft_count):
    rows_dev = q_latent.shape[0]
    owners = lax.axis_size("tensor")
    replicas = lax.axis_size("replica")
    placed = mix_call(
        q_latent, q_gain, q_up, w_uk, w_uv, w_o, new_kv, latent_cache, cache_len, draft_count,
        owners, replicas
    )
    placed = jnp.swapaxes(placed, 0, 1).reshape(rows_dev, replicas * w_o.shape[1])
    return placed.astype(jnp.bfloat16)


def solution(mesh):
    return jax.shard_map(
        shards,
        mesh=mesh,
        in_specs=(
            P(("groups", "tensor", "replica"), None),
            P(),
            P(None, "tensor"),
            P("tensor", None, None),
            P("tensor", None, None),
            P("tensor", "replica"),
            P(("groups", "tensor", "replica"), None),
            P(("groups", "tensor", "replica"), None, None),
            P(("groups", "tensor", "replica")),
            P(("groups", "tensor", "replica")),
        ),
        out_specs=P(("groups", "tensor", "replica"), None),
        check_vma=False,
    )
```

```python
import functools
import math

import jax
import jax.numpy as jnp
from jax import lax
from jax.experimental import pallas as pl
from jax.experimental.pallas import tpu as pltpu
from jax.sharding import PartitionSpec as P

LATENT = 512
ROPE = 64
NOPE = 128
VDIM = 128
DRAFT = 4
REQ_DEV = 2
MESH = pl.DeviceIdType.MESH


rms_eps = 1e-06
rope_base = 50000.0


def split_axis(count):
    near = 2 if count % 2 == 0 else 1
    side = 2 if (count // near) % 2 == 0 else 1
    return near, side, count // near // side


def column_chunks(width):
    for parts in (2, 3):
        if width % (parts * 128) == 0:
            return parts
    return 1


def meet(partners):
    barrier = pltpu.get_barrier_semaphore()
    for partner in partners:
        pl.semaphore_signal(barrier, inc=1, device_id=partner, device_id_type=MESH)
    pl.semaphore_wait(barrier, len(partners))


def place():
    group = lax.axis_index("groups")
    me = lax.axis_index("tensor")
    copy = lax.axis_index("replica")
    return group, me, copy


def project(sizes, loads, hv_ref, wo_ref, out_ref, spread, wo, sent1, got1, sent2, got2, kept2, sent3,
            got3, kept3, sentx, gotx, hs, hr, s1, r1, s2, r2, s3, r3, sx, rx):
    tensors, copies, rows_dev = sizes
    near, side, far = split_axis(tensors)
    parts = column_chunks(wo_ref.shape[1])
    width = wo_ref.shape[1] // parts
    group, me, copy = place()
    c = lax.rem(me, near)
    y = lax.rem(me // near, side)
    z = me // (near * side)

    def at(z_to, y_to, c_to):
        return (group, (z_to * side + y_to) * near + c_to, copy)

    def twin(step):
        return lax.rem(copy + step, copies)

    near_peers = [at(z, y, lax.rem(c + d, near)) for d in range(1, near)]
    side_peers = [at(z, lax.rem(y + d, side), c) for d in range(1, side)]
    far_peers = [at(lax.rem(z + d, far), y, c) for d in range(1, far)]
    twin_peers = [(group, me, twin(d)) for d in range(1, copies)]
    def send(src, dst, send_sem, recv_sem, peer):
        push = pltpu.make_async_remote_copy(
            src_ref=src, dst_ref=dst, send_sem=send_sem, recv_sem=recv_sem,
            device_id=peer, device_id_type=MESH,
        )
        push.start()
        return push

    spread_out = [
        send(hv_ref, spread.at[d - 1], hs.at[d - 1], hr.at[d - 1], twin_peers[d - 1])
        for d in range(1, copies)
    ]

    pushes1, pushes2, pushes3, pushesx = {}, {}, {}, {}

    def multiply(k):
        loads[k].wait()
        weights = wo[k]
        own = jnp.dot(hv_ref[...], weights, preferred_element_type=jnp.float32)
        if k == 0:
            for push in spread_out:
                push.wait_recv()
        others = [
            jnp.dot(spread[d], weights, preferred_element_type=jnp.float32)
            for d in range(copies - 1)
        ]
        by_step = [own] + others
        if copies == 2:
            swap = copy == 1
            ordered = [jnp.where(swap, by_step[1], by_step[0]), jnp.where(swap, by_step[0], by_step[1])]
        else:
            ordered = []
            for slot in range(copies):
                chosen = by_step[0]
                for d in range(1, copies):
                    chosen = jnp.where(lax.rem(copy - d + copies, copies) == slot, by_step[d], chosen)
                ordered.append(chosen)
        for t in range(tensors):
            block = jnp.concatenate([o[t * rows_dev : (t + 1) * rows_dev] for o in ordered], axis=0)
            ct, yt, zt = t % near, (t // near) % side, t // (near * side)
            sent1[k, ct, yt, zt] = block.astype(jnp.bfloat16)
        pushes1[k] = [
            send(sent1.at[k, lax.rem(c + d, near)], got1.at[k, d - 1],
                 s1.at[k, d - 1], r1.at[k, d - 1], near_peers[d - 1])
            for d in range(1, near)
        ]

    def sum_near(k):
        for push in pushes1[k]:
            push.wait_recv()
        for d in range(side):
            to = lax.rem(y + d, side)
            total = sent1[k, c, to].astype(jnp.float32)
            for e in range(near - 1):
                total = total + got1[k, e, to].astype(jnp.float32)
            if d == 0:
                kept2[k] = total
            else:
                sent2[k, d - 1] = total.astype(jnp.bfloat16)
        pushes2[k] = [
            send(sent2.at[k, d - 1], got2.at[k, d - 1], s2.at[k, d - 1], r2.at[k, d - 1],
                 side_peers[d - 1])
            for d in range(1, side)
        ]

    def sum_side(k):
        for push in pushes2[k]:
            push.wait_recv()
        pushes3[k] = []
        for d in list(range(1, far)) + [0]:
            to = lax.rem(z + d, far)
            total = kept2[k, to]
            for e in range(side - 1):
                total = total + got2[k, e, to].astype(jnp.float32)
            if d == 0:
                kept3[k] = total
            else:
                sent3[k, d - 1] = total.astype(jnp.bfloat16)
                pushes3[k].append(
                    send(sent3.at[k, d - 1], got3.at[k, d - 1], s3.at[k, d - 1],
                         r3.at[k, d - 1], far_peers[d - 1])
                )

    def sum_far(k):
        for push in pushes3[k]:
            push.wait_recv()
        total = kept3[k]
        for e in range(far - 1):
            total = total + got3[k, e].astype(jnp.float32)
        for r in range(copies):
            sentx[k, r] = total[r * rows_dev : (r + 1) * rows_dev]
        pushesx[k] = [
            send(sentx.at[k, twin(d)], gotx.at[k, d - 1], sx.at[k, d - 1], rx.at[k, d - 1],
                 twin_peers[d - 1])
            for d in range(1, copies)
        ]
        out_ref[copy, :, k * width : (k + 1) * width] = sentx[k, copy]

    def finish(k):
        for d in range(1, copies):
            pushesx[k][d - 1].wait_recv()
            origin = lax.rem(copy - d + copies, copies)
            out_ref[origin, :, k * width : (k + 1) * width] = gotx[k, d - 1]

    stages = (multiply, sum_near, sum_side, sum_far, finish)
    for step in range(parts + len(stages) - 1):
        for depth, stage in enumerate(stages):
            if 0 <= step - depth < parts:
                stage(step - depth)
    for push in spread_out:
        push.wait_send()
    for table in (pushes1, pushes2, pushes3, pushesx):
        for k in range(parts):
            for push in table[k]:
                push.wait_send()


def project_scratch(hv_shape, wo_shape, tensors, copies, rows_dev):
    near, side, far = split_axis(tensors)
    parts = column_chunks(wo_shape[1])
    width = wo_shape[1] // parts
    block = copies * rows_dev
    bf16, f32 = jnp.bfloat16, jnp.float32
    dma = pltpu.SemaphoreType.DMA
    n1, n2, n3, nx = (max(v - 1, 1) for v in (near, side, far, copies))
    return [
            pltpu.VMEM((nx,) + hv_shape, bf16),
            pltpu.VMEM((parts, wo_shape[0], width), bf16),
            pltpu.VMEM((parts, near, side, far, block, width), bf16),
            pltpu.VMEM((parts, n1, side, far, block, width), bf16),
            pltpu.VMEM((parts, n2, far, block, width), bf16),
            pltpu.VMEM((parts, n2, far, block, width), bf16),
            pltpu.VMEM((parts, far, block, width), f32),
            pltpu.VMEM((parts, n3, block, width), bf16),
            pltpu.VMEM((parts, n3, block, width), bf16),
            pltpu.VMEM((parts, block, width), f32),
            pltpu.VMEM((parts, copies, rows_dev, width), f32),
            pltpu.VMEM((parts, nx, rows_dev, width), f32),
            dma((nx,)), dma((nx,)),
            dma((parts, n1)), dma((parts, n1)),
            dma((parts, n2)), dma((parts, n2)),
            dma((parts, n3)), dma((parts, n3)),
            dma((parts, nx)), dma((parts, nx)),
    ]


def paired(first, second, low):
    rows = first.shape[0]
    zero = jnp.where(low, first, pltpu.roll(second, DRAFT, 0))
    one = jnp.where(low, pltpu.roll(first, rows - DRAFT, 0), second)
    return zero, one


def mix(sizes, gain_ref, ql_ref, nk_ref, len_ref, count_ref, qup_hbm, wuk_hbm, wuv_hbm, cache_hbm,
        wo_hbm, out_ref, qup, wuk, wuv, cache, hv_ref, gathered,
        qsend, rsend, qgot, rgot, lsend, lgot, load_sem, wo_sem, fs, fr, ys, yr, ns, nr, qs, qr, rs,
        rr, ls, lr, *rest):
    tensors, copies, rows_dev = sizes
    near, side, far = split_axis(tensors)
    heads_dev = wuk.shape[0]
    rows = tensors * rows_dev
    half = ql_ref.shape[1] // 2
    group, me, copy = place()
    c = lax.rem(me, near)
    y = lax.rem(me // near, side)
    z = me // (near * side)
    f32, bf16 = jnp.float32, jnp.bfloat16

    loads = [
        pltpu.make_async_copy(src, dst, load_sem.at[n])
        for n, (src, dst) in enumerate(
            ((qup_hbm, qup), (wuk_hbm, wuk), (cache_hbm, cache), (wuv_hbm, wuv))
        )
    ]
    wo = rest[1]
    width = wo.shape[2]
    wo_loads = [
        pltpu.make_async_copy(wo_hbm.at[:, pl.ds(k * width, width)], wo.at[k], wo_sem.at[k])
        for k in range(wo.shape[0])
    ]
    for load in loads + wo_loads:
        load.start()

    def peer(step):
        return lax.rem(me + step, tensors)

    def at(z_to, y_to, c_to):
        return (group, (z_to * side + y_to) * near + c_to, copy)

    def send(src, dst, send_sem, recv_sem, to):
        push = pltpu.make_async_remote_copy(
            src_ref=src, dst_ref=dst, send_sem=send_sem, recv_sem=recv_sem,
            device_id=to, device_id_type=MESH,
        )
        push.start()
        return push

    values = ql_ref[...].astype(f32)
    scaled = values * lax.rsqrt(jnp.mean(values * values, axis=-1, keepdims=True) + rms_eps)
    normed = scaled * gain_ref[...].reshape(1, 2 * half)
    gathered[c, y, z] = jnp.concatenate([normed[:, :half], normed[:, half:]], axis=0).astype(bf16)
    meet(
        [(group, peer(d), copy) for d in range(1, tensors)]
        + [(group, me, lax.rem(copy + d, copies)) for d in range(1, copies)]
    )

    far_out = [
        send(gathered.at[c, y, z], gathered.at[c, y, z], fs.at[d - 1], fr.at[d - 1],
             at(lax.rem(z + d, far), y, c))
        for d in range(1, far)
    ]
    column = lax.broadcasted_iota(jnp.int32, (rows_dev, 2 * ROPE), 1)
    table_draft = lax.broadcasted_iota(jnp.int32, (rows_dev, 2 * ROPE), 0) % DRAFT
    fraction = (column % (ROPE // 2)).astype(f32) * 2.0 / ROPE
    frequency = jnp.exp(fraction * -math.log(rope_base))
    length = jnp.where(column < ROPE, len_ref[0], len_ref[1])
    angle = (length + table_draft).astype(f32) * frequency
    cosine = jnp.cos(angle)
    sine = jnp.sin(angle)
    sine = jnp.where(column % ROPE < ROPE // 2, -sine, sine)
    for push in far_out:
        push.wait_recv()
    side_out = [
        send(gathered.at[c, y], gathered.at[c, y], ys.at[d - 1], yr.at[d - 1],
             at(z, lax.rem(y + d, side), c))
        for d in range(1, side)
    ]
    for push in side_out:
        push.wait_recv()
    near_out = [
        send(gathered.at[c], gathered.at[c], ns.at[d - 1], nr.at[d - 1],
             at(z, y, lax.rem(c + d, near)))
        for d in range(1, near)
    ]
    loads[0].wait()
    loads[1].wait()
    for push in near_out:
        push.wait_recv()

    everyone = gathered[...].astype(f32).reshape(tensors, 2 * rows_dev, half)
    left = everyone[:, :rows_dev].reshape(rows, half).astype(bf16)
    right = everyone[:, rows_dev:].reshape(rows, half).astype(bf16)
    query = jnp.dot(left, qup[:half], preferred_element_type=f32)
    query = query + jnp.dot(right, qup[half:], preferred_element_type=f32)
    query = query.astype(bf16).astype(f32)
    low = lax.broadcasted_iota(jnp.int32, (rows, 1), 0) % rows_dev < DRAFT
    qkd = NOPE + ROPE
    nope_pairs, rope_pairs = [], []
    for h in range(0, heads_dev, 2):
        here, there = h * qkd, (h + 1) * qkd
        nope_pairs.append(
            paired(query[:, here : here + NOPE], query[:, there : there + NOPE], low)
        )
        zero, one = paired(
            query[:, here + NOPE : here + qkd], query[:, there + NOPE : there + qkd], low
        )
        rope_pairs.append(jnp.concatenate([zero, one], axis=1).reshape(tensors, rows_dev, 2 * ROPE))
    rsend[...] = jnp.concatenate(rope_pairs, axis=1).astype(bf16)

    def slot(to):
        return (lax.rem(to, near) * side + lax.rem(to // near, side)) * far + to // (near * side)

    mine = slot(me)
    rope_out, query_out, latent_out = [], [], []
    for r in range(REQ_DEV):
        tiles = []
        for n, pair in enumerate(nope_pairs):
            tile = pair[r].astype(bf16)
            first = jnp.dot(tile, wuk[2 * n], preferred_element_type=f32)
            second = jnp.dot(tile, wuk[2 * n + 1], preferred_element_type=f32)
            tiles.append(jnp.where(low, first, second).reshape(tensors, rows_dev, LATENT))
        qsend[:, r] = jnp.concatenate(tiles, axis=1).astype(bf16)
        for d in range(1, tensors):
            to = peer(d)
            if r == 0:
                rope_out.append(
                    send(rsend.at[slot(to)], rgot.at[me], rs.at[d - 1], rr.at[d - 1],
                         (group, to, copy))
                )
            query_out.append(
                send(qsend.at[slot(to), r], qgot.at[me, r], qs.at[r, d - 1], qr.at[r, d - 1],
                     (group, to, copy))
            )
        qgot[me, r] = qsend[mine, r]
    rgot[me] = rsend[mine]

    pad = 128 - nk_ref.shape[0]
    fresh = jnp.concatenate(
        [nk_ref[...].astype(f32), jnp.zeros((pad, nk_ref.shape[1]), f32)], axis=0
    ).astype(bf16)
    fresh_latent, fresh_rope = fresh[:, :LATENT], fresh[:, LATENT:]
    scale = qkd ** (-0.5)
    total = tensors * heads_dev * DRAFT
    slots = cache.shape[2]
    row_draft = lax.broadcasted_iota(jnp.int32, (total, 1), 0) % DRAFT
    fresh_column = lax.broadcasted_iota(jnp.int32, (1, 128), 1)
    cache_column = lax.broadcasted_iota(jnp.int32, (1, slots), 1)
    for push in rope_out:
        push.wait_recv()
    rope = rgot[...].astype(f32).reshape(total // rows_dev, rows_dev, 2 * ROPE)
    rope2 = rope.reshape(total, 2 * ROPE)
    lane = lax.broadcasted_iota(jnp.int32, (1, 2 * ROPE), 1) % ROPE
    swapped = jnp.where(
        lane < ROPE // 2,
        pltpu.roll(rope2, 2 * ROPE - ROPE // 2, 1),
        pltpu.roll(rope2, ROPE // 2, 1),
    ).reshape(rope.shape)
    turned = (rope * cosine[None] + swapped * sine[None]).astype(bf16)
    turned = turned.reshape(total, 2 * ROPE)
    loads[2].wait()
    transposed = (((1,), (1,)), ((), ()))
    for r in range(REQ_DEV):
        for push in query_out[r * (tensors - 1) : (r + 1) * (tensors - 1)]:
            push.wait_recv()
        absorbed = qgot[:, r].reshape(total, LATENT)
        rotated = turned[:, r * ROPE : (r + 1) * ROPE]
        scores = jnp.dot(absorbed, cache[r, :LATENT], preferred_element_type=f32)
        scores = (scores + jnp.dot(rotated, cache[r, LATENT:], preferred_element_type=f32)) * scale
        fresh_scores = lax.dot_general(
            absorbed, fresh_latent, transposed, preferred_element_type=f32
        )
        fresh_scores = (
            fresh_scores
            + lax.dot_general(rotated, fresh_rope, transposed, preferred_element_type=f32)
        ) * scale
        scores = jnp.where(cache_column < len_ref[r], scores, -jnp.inf)
        begin = r * DRAFT
        seen = (fresh_column >= begin) & (fresh_column - begin <= row_draft)
        fresh_scores = jnp.where(seen, fresh_scores, -jnp.inf)
        peak = jnp.maximum(
            jnp.max(scores, axis=1, keepdims=True), jnp.max(fresh_scores, axis=1, keepdims=True)
        )
        powers = jnp.exp(scores - peak)
        fresh_powers = jnp.exp(fresh_scores - peak)
        denominator = jnp.sum(powers, axis=1, keepdims=True) + jnp.sum(
            fresh_powers, axis=1, keepdims=True
        )
        weights = (powers / denominator).astype(bf16)
        fresh_weights = (fresh_powers / denominator).astype(bf16)
        latents = lax.dot_general(
            weights, cache[r, :LATENT], transposed, preferred_element_type=f32
        )
        latents = latents + jnp.dot(fresh_weights, fresh_latent, preferred_element_type=f32)
        latents = jnp.where(row_draft < count_ref[r], latents, 0.0)
        lsend[:, r] = latents.astype(bf16).reshape(tensors, heads_dev * DRAFT, LATENT)
        for d in range(1, tensors):
            to = peer(d)
            latent_out.append(
                send(lsend.at[to, r], lgot.at[me, r], ls.at[r, d - 1], lr.at[r, d - 1],
                     (group, to, copy))
            )
        lgot[me, r] = lsend[me, r]
    loads[3].wait()
    halves = []
    for r in range(REQ_DEV):
        for push in latent_out[r * (tensors - 1) : (r + 1) * (tensors - 1)]:
            push.wait_recv()
        back = lgot[:, r].astype(f32)
        parts = []
        for n in range(heads_dev // 2):
            tile = back[:, n * rows_dev : (n + 1) * rows_dev].reshape(rows, LATENT).astype(bf16)
            first = jnp.dot(tile, wuv[2 * n], preferred_element_type=f32)
            second = jnp.dot(tile, wuv[2 * n + 1], preferred_element_type=f32)
            parts.append(jnp.where(low, first, second))
        halves.append(parts)
    for n in range(heads_dev // 2):
        for h, block in enumerate(paired(halves[0][n], halves[1][n], low)):
            start = (2 * n + h) * VDIM
            hv_ref[:, start : start + VDIM] = block.astype(bf16)
    project(sizes, wo_loads, hv_ref, wo_hbm, out_ref, *rest)
    for push in far_out + side_out + near_out + rope_out + query_out + latent_out:
        push.wait_send()


def mix_call(q_latent, q_gain, q_up, w_uk, w_uv, w_o, new_kv, latent_cache, cache_len, draft_count,
             tensors, copies):
    near, side, far = split_axis(tensors)
    rows_dev, width = q_latent.shape
    heads_dev = w_uk.shape[0]
    bf16, f32 = jnp.bfloat16, jnp.float32
    dma = pltpu.SemaphoreType.DMA
    n1, n2, n3 = (max(v - 1, 1) for v in (near, side, far))
    tall = heads_dev * DRAFT
    cache = jnp.swapaxes(latent_cache, 1, 2)
    vmem = pl.BlockSpec(memory_space=pltpu.VMEM)
    hbm = pl.BlockSpec(memory_space=pltpu.HBM)
    hv_shape = (tensors * rows_dev, heads_dev * VDIM)
    exchange = (REQ_DEV, tensors - 1)
    return pl.pallas_call(
        functools.partial(mix, (tensors, copies, rows_dev)),
        out_shape=jax.ShapeDtypeStruct((copies, rows_dev, w_o.shape[1]), f32),
        in_specs=[vmem] * 3 + [pl.BlockSpec(memory_space=pltpu.SMEM)] * 2 + [hbm] * 5,
        out_specs=vmem,
        scratch_shapes=[
            pltpu.VMEM(q_up.shape, bf16),
            pltpu.VMEM(w_uk.shape, bf16),
            pltpu.VMEM(w_uv.shape, bf16),
            pltpu.VMEM(cache.shape, bf16),
            pltpu.VMEM(hv_shape, bf16),
            pltpu.VMEM((near, side, far, 2 * rows_dev, width // 2), bf16),
            pltpu.VMEM((tensors, REQ_DEV, tall, LATENT), bf16),
            pltpu.VMEM((tensors, tall, 2 * ROPE), bf16),
            pltpu.VMEM((tensors, REQ_DEV, tall, LATENT), bf16),
            pltpu.VMEM((tensors, tall, 2 * ROPE), bf16),
            pltpu.VMEM((tensors, REQ_DEV, tall, LATENT), bf16),
            pltpu.VMEM((tensors, REQ_DEV, tall, LATENT), bf16),
            dma((4,)),
            dma((column_chunks(w_o.shape[1]),)),
            dma((n3,)), dma((n3,)),
            dma((n2,)), dma((n2,)),
            dma((n1,)), dma((n1,)),
            dma(exchange), dma(exchange),
            dma((tensors - 1,)), dma((tensors - 1,)),
            dma(exchange), dma(exchange),
        ]
        + project_scratch(hv_shape, w_o.shape, tensors, copies, rows_dev),
        compiler_params=pltpu.CompilerParams(
            collective_id=1, has_side_effects=True, vmem_limit_bytes=56 * 1024 * 1024
        ),
    )(q_gain, q_latent, new_kv, cache_len, draft_count, q_up, w_uk, w_uv, cache, w_o)


def shards(q_latent, q_gain, q_up, w_uk, w_uv, w_o, new_kv, latent_cache, cache_len, draft_count):
    rows_dev = q_latent.shape[0]
    owners = lax.axis_size("tensor")
    replicas = lax.axis_size("replica")
    placed = mix_call(
        q_latent, q_gain, q_up, w_uk, w_uv, w_o, new_kv, latent_cache, cache_len, draft_count,
        owners, replicas
    )
    placed = jnp.swapaxes(placed, 0, 1).reshape(rows_dev, replicas * w_o.shape[1])
    return placed.astype(jnp.bfloat16)


def solution(mesh):
    return jax.shard_map(
        shards,
        mesh=mesh,
        in_specs=(
            P(("groups", "tensor", "replica"), None),
            P(),
            P(None, "tensor"),
            P("tensor", None, None),
            P("tensor", None, None),
            P("tensor", "replica"),
            P(("groups", "tensor", "replica"), None),
            P(("groups", "tensor", "replica"), None, None),
            P(("groups", "tensor", "replica")),
            P(("groups", "tensor", "replica")),
        ),
        out_specs=P(("groups", "tensor", "replica"), None),
        check_vma=False,
    )
```
